32 devices in a mesh: shard: 8 (over z, x), ctx: 4 (over y, core).
Axes of the slice: x: 2, y: 2, z: 4, core: 2. Of those that a mesh axis runs over, the one named last changes fastest.
Arguments:
- inputs: bfloat16 [8, 768, 768], P('shard', 'ctx'), may hold values from -6 to 6
- encoder_states: bfloat16 [8, 512, 768], P('shard', 'ctx'), may hold values from -6 to 6
- cotangent: bfloat16 [8, 768, 768], P('shard', 'ctx'), may hold values from -6 to 6
- span_order: int32 [8], replicated, may hold values from 0 to 7, each once
- buckets: int32 [128], replicated, may hold values from 0 to 30, as said below
- gain_self: bfloat16 [768], P(('shard', 'ctx')), may hold values from 0.25 to 1.75
- self_query: bfloat16 [768, 768], P(('shard', 'ctx')), may hold values from -0.21875 to 0.21875
- self_key: bfloat16 [768, 768], P(('shard', 'ctx')), may hold values from -0.21875 to 0.21875
- self_value: bfloat16 [768, 768], P(('shard', 'ctx')), may hold values from -0.21875 to 0.21875
- self_out: bfloat16 [768, 768], P(('shard', 'ctx')), may hold values from -1.75 to 1.75
- gain_cross: bfloat16 [768], P(('shard', 'ctx')), may hold values from 0.25 to 1.75
- cross_query: bfloat16 [768, 768], P(('shard', 'ctx')), may hold values from -0.21875 to 0.21875
- cross_key: bfloat16 [768, 768], P(('shard', 'ctx')), may hold values from -0.21875 to 0.21875
- cross_value: bfloat16 [768, 768], P(('shard', 'ctx')), may hold values from -0.21875 to 0.21875
- cross_out: bfloat16 [768, 768], P(('shard', 'ctx')), may hold values from -1.75 to 1.75
- gain_feed: bfloat16 [768], P(('shard', 'ctx')), may hold values from 0.25 to 1.75
- feed_gate: bfloat16 [768, 2048], P(('shard', 'ctx')), may hold values from -0.21875 to 0.21875
- feed_up: bfloat16 [768, 2048], P(('shard', 'ctx')), may hold values from -0.21875 to 0.21875
- feed_down: bfloat16 [2048, 768], P(('shard', 'ctx')), may hold values from -0.125 to 0.125
- bias_table: float32 [32, 12], replicated, may hold values from -6 to 6
Outputs:
- outputs: bfloat16 [8, 768, 768], P('shard', 'ctx')
- input_grad: bfloat16 [8, 768, 768], P('shard', 'ctx')
- encoder_grad: bfloat16 [8, 512, 768], P('shard', 'ctx')
- gain_self_grad: float32 [768], P(('shard', 'ctx'))
- self_query_grad: float32 [768, 768], P(('shard', 'ctx'))
- self_key_grad: float32 [768, 768], P(('shard', 'ctx'))
- self_value_grad: float32 [768, 768], P(('shard', 'ctx'))
- self_out_grad: float32 [768, 768], P(('shard', 'ctx'))
- gain_cross_grad: float32 [768], P(('shard', 'ctx'))
- cross_query_grad: float32 [768, 768], P(('shard', 'ctx'))
- cross_key_grad: float32 [768, 768], P(('shard', 'ctx'))
- cross_value_grad: float32 [768, 768], P(('shard', 'ctx'))
- cross_out_grad: float32 [768, 768], P(('shard', 'ctx'))
- gain_feed_grad: float32 [768], P(('shard', 'ctx'))
- feed_gate_grad: float32 [768, 2048], P(('shard', 'ctx'))
- feed_up_grad: float32 [768, 2048], P(('shard', 'ctx'))
- feed_down_grad: float32 [2048, 768], P(('shard', 'ctx'))
- bias_table_grad: float32 [32, 12], replicated
The draws below stay inside these ranges and needn't reach their ends.
Inputs may be any that keep to these rules, and one draw needn't show every extreme that they name: A permutation of the blocks: rows i * 96 to (i + 1) * 96 - 1 of every sequence hold the consecutive positions from span_order[i] * 96 on. A drawn monotone bucket map: buckets[0] is 0; each next entry is 1 or 2 higher until 30 is reached, then it stays there.
All inputs are finite; a program needn't handle non-finite values.
Results may differ from the reference program's by a relative error of at most 0.024.
Values may be sent and summed in bfloat16 or wider, within the bound.
No kernel may reach another device: no remote copies, remote signals or barrier semaphores. Data moves between devices by JAX's collectives and lax.ppermute only.
A program may use at most 192 MiB of HBM per device.

```python
import math
import jax
import jax.numpy as jnp
from jax import lax

D = 768
HEADS = 12
DH = 64
FF = 2048
NBUCK = 32
MAXD = 128
ENC = 512
TOK_DEV = 192
SPAN = 96
SPANS = 8
LEN = 768
SEQS = 8
N_CTX = 4


def draw_buckets(key, part):
    key = jax.random.fold_in(key, 11)
    raises = jax.random.randint(key, (MAXD,), 1, 3, dtype=jnp.int32)
    raises = jnp.where(jnp.arange(MAXD, dtype=jnp.int32) == 0, 0, raises)
    return jnp.minimum(jnp.cumsum(raises), NBUCK - 2).astype(jnp.int32)


def steps_of(key, dims, shards, least, top_value):
    level = 1.0
    for position, shards_of in shards:
        heights = jax.random.uniform(jax.random.fold_in(jax.random.fold_in(key, 6), position), (shards_of,), jnp.float32, least / len(shards), top_value / len(shards))
        level = level * jnp.repeat(jnp.exp(heights), dims[position] // shards_of).reshape((-1,) + (1,) * (len(dims) - 1 - position))
    return level


def scatter_about(key, extent, width, reach, pieces=(), kind=jnp.bfloat16):
    array = width * jax.random.normal(key, extent, jnp.float32)
    if pieces:
        array = array * steps_of(key, extent, pieces, -0.22, 0.18)
    return jnp.clip(array, -reach, reach).astype(kind)


def setup_inputs(seed: int = 0) -> dict:
    splits = jax.random.split(jax.random.key(seed), 21)
    inputs = scatter_about(splits[0], (SEQS, LEN, D), 1.0, 6.0, ((0, 8), (1, 4)))
    encoder_states = scatter_about(splits[1], (SEQS, ENC, D), 1.0, 6.0, ((0, 8), (1, 4)))
    cotangent = scatter_about(splits[2], (SEQS, LEN, D), 1.0, 6.0, ((0, 8), (1, 4)))
    span_order = jax.random.permutation(splits[3], SPANS).astype(jnp.int32)
    buckets = draw_buckets(jax.random.fold_in(splits[20], 71), 0)
    gain_self = jnp.clip(1.0 + 0.15 * jax.random.normal(splits[5], (D,), jnp.float32), 0.25, 1.75).astype(jnp.bfloat16)
    self_query = scatter_about(splits[6], (D, D), D ** -0.5, 0.21875, ((0, 32),))
    self_key = scatter_about(splits[7], (D, D), D ** -0.5, 0.21875, ((0, 32),))
    self_value = scatter_about(splits[8], (D, D), D ** -0.5, 0.21875, ((0, 32),))
    self_out = scatter_about(splits[9], (D, D), (max(1, 12 * D // (TOK_DEV * N_CTX))) ** -0.5, 1.75, ((0, 32),))
    gain_cross = jnp.clip(1.0 + 0.15 * jax.random.normal(splits[10], (D,), jnp.float32), 0.25, 1.75).astype(jnp.bfloat16)
    cross_query = scatter_about(splits[11], (D, D), D ** -0.5, 0.21875, ((0, 32),))
    cross_key = scatter_about(splits[12], (D, D), D ** -0.5, 0.21875, ((0, 32),))
    cross_value = scatter_about(splits[13], (D, D), D ** -0.5, 0.21875, ((0, 32),))
    cross_out = scatter_about(splits[14], (D, D), (max(1, D * 8 // ENC)) ** -0.5, 1.75, ((0, 32),))
    gain_feed = jnp.clip(1.0 + 0.15 * jax.random.normal(splits[15], (D,), jnp.float32), 0.25, 1.75).astype(jnp.bfloat16)
    feed_gate = scatter_about(splits[16], (D, FF), D ** -0.5, 0.21875, ((0, 32),))
    feed_up = scatter_about(splits[17], (D, FF), D ** -0.5, 0.21875, ((0, 32),))
    feed_down = scatter_about(splits[18], (FF, D), FF ** -0.5, 0.125, ((0, 32),))
    bias_table = scatter_about(splits[19], (NBUCK, HEADS), 1.0, 6.0, (), jnp.float32)
    return {"inputs": inputs, "encoder_states": encoder_states, "cotangent": cotangent, "span_order": span_order, "buckets": buckets, "gain_self": gain_self, "self_query": self_query, "self_key": self_key, "self_value": self_value, "self_out": self_out, "gain_cross": gain_cross, "cross_query": cross_query, "cross_key": cross_key, "cross_value": cross_value, "cross_out": cross_out, "gain_feed": gain_feed, "feed_gate": feed_gate, "feed_up": feed_up, "feed_down": feed_down, "bias_table": bias_table}


EPSILON = 1e-06
PRECISE = lax.Precision.HIGHEST

@jax.custom_vjp
def low(v):
    return lax.optimization_barrier(v.astype(jnp.bfloat16)).astype(jnp.float32)

@jax.custom_vjp
def low_back(v):
    return v

def low_keep(v):
    return (low(v), None)

def low_pass(kept, grad):
    return (grad,)

def back_keep(v):
    return (v, None)

def back_low(kept, grad):
    return (low(grad),)
low.defvjp(low_keep, low_pass)
low_back.defvjp(back_keep, back_low)

def normed(values, gain):
    return values * lax.rsqrt(lax.optimization_barrier(jnp.mean(values * values, axis=-1, keepdims=True)) + EPSILON) * gain

def matmul(left, right):
    return jnp.dot(left, right, precision=PRECISE)

def split_heads(matrix):
    return matrix.reshape(matrix.shape[0], HEADS, DH)

def self_block(queries, query_pos, keys, values, key_pos, dist_bias):
    scores = jnp.einsum('qhd,khd->hqk', queries, keys, precision=PRECISE) * DH ** (-0.5)
    offset = query_pos[:, None] - key_pos[None, :]
    scores = low_back(scores + jnp.take(dist_bias, jnp.clip(offset, 0, MAXD), axis=1))
    scores = jnp.where(offset >= 0, scores, -jnp.inf)
    probs = low(jax.nn.softmax(scores, axis=-1))
    return jnp.einsum('hqk,khd->qhd', probs, values, precision=PRECISE)

def forward(tokens, encoded, params, positions, dist_bucket):
    gain_self, self_query, self_key, self_value, self_out, gain_cross, cross_query, cross_key, cross_value, cross_out, gain_feed, feed_gate, feed_up, feed_down, bias_table = params
    dist_bias = jnp.take(bias_table, dist_bucket, axis=0).T
    normed_self = low(normed(tokens, gain_self))
    queries = low_back(low(matmul(normed_self, self_query)))
    keys = low_back(low(matmul(normed_self, self_key)))
    values = low_back(low(matmul(normed_self, self_value)))
    block_rows = math.gcd(512, LEN)
    block_count = LEN // block_rows
    key_heads = split_heads(keys)
    value_heads = split_heads(values)

    def one_block(item):
        return self_block(item[0], item[1], key_heads, value_heads, positions, dist_bias)
    attended = lax.map(jax.checkpoint(one_block), (split_heads(queries).reshape(block_count, block_rows, HEADS, DH), positions.reshape(block_count, block_rows)))
    attended = low_back(low(attended.reshape(LEN, D)))
    after_self = tokens + low_back(matmul(attended, self_out))
    normed_cross = low(normed(after_self, gain_cross))
    cross_q = low_back(low(matmul(normed_cross, cross_query)))
    cross_k = low_back(low(matmul(encoded, cross_key)))
    cross_v = low_back(low(matmul(encoded, cross_value)))
    cross_scores = low_back(jnp.einsum('qhd,khd->hqk', split_heads(cross_q), split_heads(cross_k), precision=PRECISE) * DH ** (-0.5))
    cross_probs = low(jax.nn.softmax(cross_scores, axis=-1))
    cross_att = jnp.einsum('hqk,khd->qhd', cross_probs, split_heads(cross_v), precision=PRECISE)
    cross_att = low_back(low(cross_att.reshape(LEN, D)))
    after_cross = after_self + low_back(matmul(cross_att, cross_out))
    normed_feed = low(normed(after_cross, gain_feed))
    gate_pre = low_back(matmul(normed_feed, feed_gate))
    up_pre = low_back(matmul(normed_feed, feed_up))
    hidden = low(jax.nn.gelu(gate_pre, approximate=True) * up_pre)
    return after_cross + low_back(matmul(hidden, feed_down))

def reference(inputs, encoder_states, cotangent, span_order, buckets, gain_self, self_query, self_key, self_value, self_out, gain_cross, cross_query, cross_key, cross_value, cross_out, gain_feed, feed_gate, feed_up, feed_down, bias_table):
    params = tuple((w.astype(jnp.float32) for w in (gain_self, self_query, self_key, self_value, self_out, gain_cross, cross_query, cross_key, cross_value, cross_out, gain_feed, feed_gate, feed_up, feed_down, bias_table)))
    row_index = jnp.arange(LEN, dtype=jnp.int32)
    positions = (span_order[row_index // SPAN] * SPAN + row_index % SPAN).astype(jnp.int32)
    dist_bucket = jnp.concatenate([buckets, jnp.full((1,), NBUCK - 1, jnp.int32)])

    def one_sequence(totals, items):
        tokens, encoded, outer = items
        result, pull = jax.vjp(lambda a, b, c: forward(a, b, c, positions, dist_bucket), tokens, encoded, params)
        grad_tokens, grad_encoded, grad_params = pull(outer)
        totals = tuple((t + g for t, g in zip(totals, grad_params)))
        return (totals, (result.astype(jnp.bfloat16), grad_tokens.astype(jnp.bfloat16), grad_encoded.astype(jnp.bfloat16)))
    start_totals = tuple((jnp.zeros_like(w) for w in params))
    grads, (outputs, input_grad, encoder_grad) = lax.scan(one_sequence, start_totals, (inputs.astype(jnp.float32), encoder_states.astype(jnp.float32), cotangent.astype(jnp.float32)))
    return (outputs, input_grad, encoder_grad, grads[0], grads[1], grads[2], grads[3], grads[4], grads[5], grads[6], grads[7], grads[8], grads[9], grads[10], grads[11], grads[12], grads[13], grads[14])
```

```python
import math

import jax
import jax.numpy as jnp
from jax import lax
from jax.sharding import PartitionSpec as P

EPSILON = 1e-06
MASKED = -1e30
PRECISE = lax.Precision.HIGHEST


def normed(values, gain):
    return values * lax.rsqrt(jnp.mean(values * values, axis=-1, keepdims=True) + EPSILON) * gain


def project(left, right):
    return jnp.dot(left, right, preferred_element_type=jnp.float32)


def project_back(grads, weight):
    return lax.dot_general(
        grads, weight, (((1,), (1,)), ((), ())), preferred_element_type=jnp.float32
    )


def outer_sum(left, grads):
    return lax.dot_general(
        left, grads, (((0,), (0,)), ((), ())), preferred_element_type=jnp.float32
    )


def split_heads(matrix, head_count):
    return matrix.reshape(matrix.shape[0], head_count, matrix.shape[1] // head_count)


def locate(span_order, first_row, row_total, span_rows):
    row_index = first_row + jnp.arange(row_total, dtype=jnp.int32)
    slot_index = row_index // span_rows
    span_slots = jnp.arange(span_order.shape[0], dtype=jnp.int32)
    chosen = jnp.sum(
        jnp.where(slot_index[:, None] == span_slots[None, :], span_order[None, :], 0), axis=1
    )
    return chosen * span_rows + row_index % span_rows


def bucket_edges(buckets, table_rows):
    levels = jnp.arange(1, table_rows, dtype=jnp.int32)
    return jnp.sum((buckets[None, :] < levels[:, None]).astype(jnp.int32), axis=1)


def scores_for(query_heads, query_pos, key_heads, key_pos, table, edges, score_scale):
    table_rows = table.shape[0]
    products = (
        jnp.einsum("qhd,khd->hqk", query_heads, key_heads, preferred_element_type=jnp.float32)
        * score_scale
    )
    offset = query_pos[:, None] - key_pos[None, :]
    bucket_index = jnp.sum((offset[:, :, None] >= edges[None, None, :]).astype(jnp.int32), axis=-1)
    onehot = (bucket_index[:, :, None] == jnp.arange(table_rows, dtype=jnp.int32)).astype(
        jnp.float32
    )
    bias = jnp.einsum("qkb,bh->hqk", onehot, table, precision=PRECISE)
    scores = jnp.where(offset >= 0, products + bias, MASKED)
    return (scores, onehot)


def key_block(matrix, block_start, block_size, head_count):
    return split_heads(lax.dynamic_slice_in_dim(matrix, block_start, block_size, 0), head_count)


def softmax_stats(query_heads, query_pos, keys_all, key_pos, table, edges, score_scale, block_size):
    head_count = query_heads.shape[1]
    query_count = query_heads.shape[0]

    def softmax_visit(running, block_start):
        running_max, exp_total = running
        key_heads = key_block(keys_all, block_start, block_size, head_count)
        key_place = lax.dynamic_slice_in_dim(key_pos, block_start, block_size, 0)
        scores, _ = scores_for(
            query_heads, query_pos, key_heads, key_place, table, edges, score_scale
        )
        highest = jnp.maximum(running_max, jnp.max(scores, axis=-1))
        exp_total = exp_total * jnp.exp(running_max - highest) + jnp.sum(
            jnp.exp(scores - highest[:, :, None]), axis=-1
        )
        return ((highest, exp_total), None)

    initial = (
        jnp.full((head_count, query_count), MASKED, jnp.float32),
        jnp.zeros((head_count, query_count), jnp.float32),
    )
    starts = jnp.arange(keys_all.shape[0] // block_size, dtype=jnp.int32) * block_size
    (running_max, exp_total), _ = lax.scan(softmax_visit, initial, starts)
    return running_max + jnp.log(exp_total)


def attend_values(
    query_heads,
    query_pos,
    keys_all,
    values_all,
    key_pos,
    table,
    edges,
    log_norm,
    score_scale,
    block_size,
):
    head_count = query_heads.shape[1]

    def attend_visit(sums, block_start):
        rounded_sum, extra_sum = sums
        key_heads = key_block(keys_all, block_start, block_size, head_count)
        value_heads = key_block(values_all, block_start, block_size, head_count)
        key_place = lax.dynamic_slice_in_dim(key_pos, block_start, block_size, 0)
        scores, _ = scores_for(
            query_heads, query_pos, key_heads, key_place, table, edges, score_scale
        )
        probs = jnp.exp(scores - log_norm[:, :, None])
        probs_low = probs.astype(jnp.bfloat16)
        remainder = (probs - probs_low.astype(jnp.float32)).astype(jnp.bfloat16)
        rounded_sum = rounded_sum + jnp.einsum(
            "hqk,khd->qhd", probs_low, value_heads, preferred_element_type=jnp.float32
        )
        extra_sum = extra_sum + jnp.einsum(
            "hqk,khd->qhd", remainder, value_heads, preferred_element_type=jnp.float32
        )
        return ((rounded_sum, extra_sum), None)

    zeros_like_out = jnp.zeros(query_heads.shape, jnp.float32)
    starts = jnp.arange(keys_all.shape[0] // block_size, dtype=jnp.int32) * block_size
    (rounded_sum, extra_sum), _ = lax.scan(attend_visit, (zeros_like_out, zeros_like_out), starts)
    return (rounded_sum, rounded_sum + extra_sum)


def self_backward(
    query_heads,
    grad_heads,
    query_pos,
    keys_all,
    values_all,
    key_pos,
    table,
    edges,
    log_norm,
    delta,
    score_scale,
    block_size,
):
    head_count = query_heads.shape[1]
    table_rows = table.shape[0]

    def self_visit(sums, block_start):
        grad_query, grad_table = sums
        key_heads = key_block(keys_all, block_start, block_size, head_count)
        value_heads = key_block(values_all, block_start, block_size, head_count)
        key_place = lax.dynamic_slice_in_dim(key_pos, block_start, block_size, 0)
        scores, onehot = scores_for(
            query_heads, query_pos, key_heads, key_place, table, edges, score_scale
        )
        probs = jnp.exp(scores - log_norm[:, :, None])
        grad_probs = jnp.einsum(
            "qhd,khd->hqk", grad_heads, value_heads, preferred_element_type=jnp.float32
        )
        grad_scores = (probs * (grad_probs - delta[:, :, None])).astype(jnp.bfloat16)
        grad_query = grad_query + jnp.einsum(
            "hqk,khd->qhd", grad_scores, key_heads, preferred_element_type=jnp.float32
        )
        grad_table = grad_table + jnp.einsum(
            "hqk,qkb->bh",
            grad_scores,
            onehot.astype(jnp.bfloat16),
            preferred_element_type=jnp.float32,
        )
        probs_low = probs.astype(jnp.bfloat16)
        grad_key = jnp.einsum(
            "hqk,qhd->khd", grad_scores, query_heads, preferred_element_type=jnp.float32
        )
        grad_value = jnp.einsum(
            "hqk,qhd->khd", probs_low, grad_heads, preferred_element_type=jnp.float32
        )
        return ((grad_query, grad_table), (grad_key, grad_value))

    initial = (
        jnp.zeros(query_heads.shape, jnp.float32),
        jnp.zeros((table_rows, head_count), jnp.float32),
    )
    starts = jnp.arange(keys_all.shape[0] // block_size, dtype=jnp.int32) * block_size
    return lax.scan(self_visit, initial, starts)


def per_device(
    inputs,
    encoder_states,
    cotangent,
    span_order,
    buckets,
    gain_self,
    self_query,
    self_key,
    self_value,
    self_out,
    gain_cross,
    cross_query,
    cross_key,
    cross_value,
    cross_out,
    gain_feed,
    feed_gate,
    feed_up,
    feed_down,
    bias_table,
):
    squares = (
        self_query,
        self_key,
        self_value,
        self_out,
        cross_query,
        cross_key,
        cross_value,
        cross_out,
        feed_gate,
        feed_up,
    )
    gains = jnp.stack((gain_self, gain_cross, gain_feed), axis=1)
    gains = jnp.pad(gains, ((0, 0), (0, 128 - gains.shape[1])))
    packed = lax.all_gather(
        jnp.concatenate(squares + (gains,), axis=1), ("shard", "ctx"), axis=0, tiled=True
    )
    whole_feed_down = lax.all_gather(feed_down, ("shard", "ctx"), axis=0, tiled=True)
    unpacked = []
    start = 0
    for part in squares:
        unpacked.append(lax.slice_in_dim(packed, start, start + part.shape[1], axis=1))
        start += part.shape[1]
    (
        whole_self_query,
        whole_self_key,
        whole_self_value,
        whole_self_out,
        whole_cross_query,
        whole_cross_key,
        whole_cross_value,
        whole_cross_out,
        whole_feed_gate,
        whole_feed_up,
    ) = unpacked
    gain_rows = lax.slice_in_dim(packed, start, start + 128, axis=1).T
    whole_gain_self, whole_gain_cross, whole_gain_feed = gain_rows[0], gain_rows[1], gain_rows[2]
    token_rows = inputs.shape[1]
    width = inputs.shape[2]
    head_count = bias_table.shape[1]
    head_size = width // head_count
    table_rows = bias_table.shape[0]
    group_size = lax.axis_size("ctx")
    device_slot = lax.axis_index("ctx")
    seq_rows = token_rows * group_size
    span_rows = token_rows // 2
    block_size = math.gcd(512, seq_rows)
    score_scale = head_size ** (-0.5)
    query_pos = locate(span_order, device_slot * token_rows, token_rows, span_rows)
    key_pos = locate(span_order, 0, seq_rows, span_rows)
    edges = bucket_edges(buckets, table_rows)
    tokens = inputs[0].astype(jnp.float32)
    normed_self = normed(tokens, whole_gain_self.astype(jnp.float32)).astype(jnp.bfloat16)
    queries = project(normed_self, whole_self_query).astype(jnp.bfloat16)
    keys_local = project(normed_self, whole_self_key).astype(jnp.bfloat16)
    values_local = project(normed_self, whole_self_value).astype(jnp.bfloat16)
    keys_all, values_all = (
        lax.all_gather(keys_local, "ctx", axis=0, tiled=True),
        lax.all_gather(values_local, "ctx", axis=0, tiled=True),
    )
    query_heads = split_heads(queries, head_count)
    log_self = softmax_stats(
        query_heads, query_pos, keys_all, key_pos, bias_table, edges, score_scale, block_size
    )
    self_rounded, self_exact = attend_values(
        query_heads,
        query_pos,
        keys_all,
        values_all,
        key_pos,
        bias_table,
        edges,
        log_self,
        score_scale,
        block_size,
    )
    attended = self_rounded.reshape(token_rows, width).astype(jnp.bfloat16)
    after_self = tokens + project(attended, whole_self_out)
    normed_cross = normed(after_self, whole_gain_cross.astype(jnp.float32)).astype(jnp.bfloat16)
    cross_q = project(normed_cross, whole_cross_query).astype(jnp.bfloat16)
    encoded_local = encoder_states[0]
    encoded_all = lax.all_gather(encoded_local, "ctx", axis=0, tiled=True)
    cross_k = project(encoded_all, whole_cross_key).astype(jnp.bfloat16)
    cross_v = project(encoded_all, whole_cross_value).astype(jnp.bfloat16)
    cross_q_heads = split_heads(cross_q, head_count)
    cross_k_heads = split_heads(cross_k, head_count)
    cross_v_heads = split_heads(cross_v, head_count)
    cross_scores = (
        jnp.einsum("qhd,khd->hqk", cross_q_heads, cross_k_heads, preferred_element_type=jnp.float32)
        * score_scale
    )
    cross_top = jnp.max(cross_scores, axis=-1)
    log_cross = cross_top + jnp.log(jnp.sum(jnp.exp(cross_scores - cross_top[:, :, None]), axis=-1))
    cross_probs = jnp.exp(cross_scores - log_cross[:, :, None])
    cross_low = cross_probs.astype(jnp.bfloat16)
    cross_remainder = (cross_probs - cross_low.astype(jnp.float32)).astype(jnp.bfloat16)
    cross_rounded = jnp.einsum(
        "hqk,khd->qhd", cross_low, cross_v_heads, preferred_element_type=jnp.float32
    )
    cross_exact = cross_rounded + jnp.einsum(
        "hqk,khd->qhd", cross_remainder, cross_v_heads, preferred_element_type=jnp.float32
    )
    cross_att = cross_rounded.reshape(token_rows, width).astype(jnp.bfloat16)
    after_cross = after_self + project(cross_att, whole_cross_out)
    normed_feed = normed(after_cross, whole_gain_feed.astype(jnp.float32)).astype(jnp.bfloat16)
    gate_pre = project(normed_feed, whole_feed_gate)
    up_pre = project(normed_feed, whole_feed_up)
    gated, gated_pull = jax.vjp(
        lambda first, second: jax.nn.gelu(first, approximate=True) * second, gate_pre, up_pre
    )
    hidden = gated.astype(jnp.bfloat16)
    outputs = (after_cross + project(hidden, whole_feed_down)).astype(jnp.bfloat16)
    outer = cotangent[0].astype(jnp.float32)
    grad_feed_out = outer.astype(jnp.bfloat16)
    down_grad = outer_sum(hidden, grad_feed_out)
    grad_hidden = project_back(grad_feed_out, whole_feed_down)
    grad_gate_f, grad_up_f = gated_pull(grad_hidden)
    grad_gate = grad_gate_f.astype(jnp.bfloat16)
    grad_up = grad_up_f.astype(jnp.bfloat16)
    gate_grad = outer_sum(normed_feed, grad_gate)
    up_grad = outer_sum(normed_feed, grad_up)
    grad_normed_feed = project_back(grad_gate, whole_feed_gate) + project_back(grad_up, whole_feed_up)
    _, feed_norm_pull = jax.vjp(normed, after_cross, whole_gain_feed.astype(jnp.float32))
    grad_after_feed, gain_feed_grad = feed_norm_pull(grad_normed_feed)
    grad_after_cross = outer + grad_after_feed
    grad_cross_branch = grad_after_cross.astype(jnp.bfloat16)
    cross_out_grad = outer_sum(cross_att, grad_cross_branch)
    grad_cross_att = project_back(grad_cross_branch, whole_cross_out).astype(jnp.bfloat16)
    grad_cross_heads = split_heads(grad_cross_att, head_count)
    cross_delta = jnp.sum(
        (grad_cross_att.astype(jnp.float32) * cross_exact.reshape(token_rows, width)).reshape(
            token_rows, head_count, head_size
        ),
        axis=-1,
    ).T
    cross_grad_probs = jnp.einsum(
        "qhd,khd->hqk", grad_cross_heads, cross_v_heads, preferred_element_type=jnp.float32
    )
    cross_grad_scores = (cross_probs * (cross_grad_probs - cross_delta[:, :, None])).astype(
        jnp.bfloat16
    )
    grad_cross_q = (
        (
            jnp.einsum(
                "hqk,khd->qhd", cross_grad_scores, cross_k_heads, preferred_element_type=jnp.float32
            )
            * score_scale
        )
        .reshape(token_rows, width)
        .astype(jnp.bfloat16)
    )
    part_cross_k = (
        jnp.einsum(
            "hqk,qhd->khd", cross_grad_scores, cross_q_heads, preferred_element_type=jnp.float32
        )
        * score_scale
    ).reshape(-1, width)
    part_cross_v = jnp.einsum(
        "hqk,qhd->khd", cross_low, grad_cross_heads, preferred_element_type=jnp.float32
    ).reshape(-1, width)
    summed_cross_k, summed_cross_v = (
        lax.psum_scatter(
            part_cross_k.astype(jnp.bfloat16), "ctx", scatter_dimension=0, tiled=True
        ).astype(jnp.float32),
        lax.psum_scatter(
            part_cross_v.astype(jnp.bfloat16), "ctx", scatter_dimension=0, tiled=True
        ).astype(jnp.float32),
    )
    grad_cross_k = summed_cross_k.astype(jnp.bfloat16)
    grad_cross_v = summed_cross_v.astype(jnp.bfloat16)
    cross_key_grad = outer_sum(encoded_local, grad_cross_k)
    cross_value_grad = outer_sum(encoded_local, grad_cross_v)
    encoder_grad = (
        project_back(grad_cross_k, whole_cross_key) + project_back(grad_cross_v, whole_cross_value)
    ).astype(jnp.bfloat16)
    cross_query_grad = outer_sum(normed_cross, grad_cross_q)
    grad_normed_cross = project_back(grad_cross_q, whole_cross_query)
    _, cross_norm_pull = jax.vjp(normed, after_self, whole_gain_cross.astype(jnp.float32))
    grad_after_norm, gain_cross_grad = cross_norm_pull(grad_normed_cross)
    grad_after_self = grad_after_cross + grad_after_norm
    grad_self_branch = grad_after_self.astype(jnp.bfloat16)
    self_out_grad = outer_sum(attended, grad_self_branch)
    grad_attended = project_back(grad_self_branch, whole_self_out).astype(jnp.bfloat16)
    grad_heads = split_heads(grad_attended, head_count)
    self_delta = jnp.sum(
        (grad_attended.astype(jnp.float32) * self_exact.reshape(token_rows, width)).reshape(
            token_rows, head_count, head_size
        ),
        axis=-1,
    ).T
    (grad_query_f, table_part), stacked = self_backward(
        query_heads,
        grad_heads,
        query_pos,
        keys_all,
        values_all,
        key_pos,
        bias_table,
        edges,
        log_self,
        self_delta,
        score_scale,
        block_size,
    )
    part_keys = (stacked[0] * score_scale).reshape(seq_rows, width)
    part_values = stacked[1].reshape(seq_rows, width)
    summed_key, summed_value = (
        lax.psum_scatter(
            part_keys.astype(jnp.bfloat16), "ctx", scatter_dimension=0, tiled=True
        ).astype(jnp.float32),
        lax.psum_scatter(
            part_values.astype(jnp.bfloat16), "ctx", scatter_dimension=0, tiled=True
        ).astype(jnp.float32),
    )
    grad_query = (grad_query_f * score_scale).reshape(token_rows, width).astype(jnp.bfloat16)
    grad_key = summed_key.astype(jnp.bfloat16)
    grad_value = summed_value.astype(jnp.bfloat16)
    query_grad = outer_sum(normed_self, grad_query)
    key_grad = outer_sum(normed_self, grad_key)
    value_grad = outer_sum(normed_self, grad_value)
    grad_normed_self = (
        project_back(grad_query, whole_self_query)
        + project_back(grad_key, whole_self_key)
        + project_back(grad_value, whole_self_value)
    )
    _, self_norm_pull = jax.vjp(normed, tokens, whole_gain_self.astype(jnp.float32))
    grad_tokens_norm, gain_self_grad = self_norm_pull(grad_normed_self)
    input_grad = (grad_after_self + grad_tokens_norm).astype(jnp.bfloat16)
    square_grads = (
        query_grad,
        key_grad,
        value_grad,
        self_out_grad,
        cross_query_grad,
        cross_key_grad,
        cross_value_grad,
        cross_out_grad,
        gate_grad,
        up_grad,
    )
    packed_grads = jnp.concatenate([g.astype(jnp.bfloat16) for g in square_grads], axis=1)
    own_packed = lax.psum_scatter(
        packed_grads, ("shard", "ctx"), scatter_dimension=0, tiled=True
    ).astype(jnp.float32)
    own_down = lax.psum_scatter(
        down_grad.astype(jnp.bfloat16), ("shard", "ctx"), scatter_dimension=0, tiled=True
    ).astype(jnp.float32)
    own = []
    start = 0
    for part in square_grads:
        own.append(lax.slice_in_dim(own_packed, start, start + part.shape[1], axis=1))
        start += part.shape[1]
    small = lax.psum(
        (gain_self_grad, gain_cross_grad, gain_feed_grad, table_part), ("shard", "ctx")
    )
    slot = lax.axis_index(("shard", "ctx"))
    own_gains = [
        lax.dynamic_slice_in_dim(g, slot * gain_self.shape[0], gain_self.shape[0], 0)
        for g in small[:3]
    ]
    return (
        outputs[None],
        input_grad[None],
        encoder_grad[None],
        own_gains[0],
        own[0],
        own[1],
        own[2],
        own[3],
        own_gains[1],
        own[4],
        own[5],
        own[6],
        own[7],
        own_gains[2],
        own[8],
        own[9],
        own_down,
        small[3],
    )


def solution(mesh):
    in_specs = (
        P("shard", "ctx", None),
        P("shard", "ctx", None),
        P("shard", "ctx", None),
        P(),
        P(),
        P(("shard", "ctx")),
        P(("shard", "ctx"), None),
        P(("shard", "ctx"), None),
        P(("shard", "ctx"), None),
        P(("shard", "ctx"), None),
        P(("shard", "ctx")),
        P(("shard", "ctx"), None),
        P(("shard", "ctx"), None),
        P(("shard", "ctx"), None),
        P(("shard", "ctx"), None),
        P(("shard", "ctx")),
        P(("shard", "ctx"), None),
        P(("shard", "ctx"), None),
        P(("shard", "ctx"), None),
        P(),
    )
    out_specs = (
        P("shard", "ctx", None),
        P("shard", "ctx", None),
        P("shard", "ctx", None),
        P(("shard", "ctx")),
        P(("shard", "ctx"), None),
        P(("shard", "ctx"), None),
        P(("shard", "ctx"), None),
        P(("shard", "ctx"), None),
        P(("shard", "ctx")),
        P(("shard", "ctx"), None),
        P(("shard", "ctx"), None),
        P(("shard", "ctx"), None),
        P(("shard", "ctx"), None),
        P(("shard", "ctx")),
        P(("shard", "ctx"), None),
        P(("shard", "ctx"), None),
        P(("shard", "ctx"), None),
        P(),
    )
    return jax.shard_map(
        per_device, mesh=mesh, in_specs=in_specs, out_specs=out_specs, check_vma=False
    )
```

```python
import functools

import jax
import jax.numpy as jnp
from jax import lax
from jax.experimental import pallas as pl
from jax.experimental.pallas import tpu as pltpu
from jax.sharding import PartitionSpec as P

EPSILON = 1e-06
MASKED = -1e30
PRECISE = lax.Precision.HIGHEST
LANES = 128
BOTH = ("shard", "ctx")
F32 = jnp.float32
BF16 = jnp.bfloat16


def inverse_norm(values):
    return lax.rsqrt(jnp.mean(values * values, axis=-1, keepdims=True) + EPSILON)


def norm_back(values, inverse, gain, grads):
    weighted = gain * grads
    middle = jnp.mean(weighted * values, axis=-1, keepdims=True)
    return inverse * weighted - values * (inverse * inverse * inverse) * middle


def project(left, right):
    return jnp.dot(left, right, preferred_element_type=F32)


def project_back(grads, weight):
    return lax.dot_general(grads, weight, (((1,), (1,)), ((), ())), preferred_element_type=F32)


def outer_sum(left, grads):
    return lax.dot_general(left, grads, (((0,), (0,)), ((), ())), preferred_element_type=F32)


def swap(values, mask):
    count = lax.axis_size("shard") * lax.axis_size("ctx")
    return lax.ppermute(values, BOTH, [(i, i ^ mask) for i in range(count)])


def pick(values, index, axis):
    return lax.dynamic_index_in_dim(values, index, axis, keepdims=False)


def paired(first, second, flag):
    joined = jnp.concatenate((first, second), axis=0)
    return jnp.where(flag == 0, joined, jnp.concatenate((second, first), axis=0))


def ctx_gather(values, quads):
    if not quads:
        return lax.all_gather(values, "ctx", axis=0, tiled=True)
    slot = lax.axis_index("ctx")
    far = swap(values, 2)
    near = paired(values, swap(values, 1), slot % 2)
    far = paired(far, swap(far, 1), slot % 2)
    return paired(near, far, slot // 2)


def ctx_scatter_sum(values, quads):
    if not quads:
        return lax.psum_scatter(values, "ctx", scatter_dimension=0, tiled=True).astype(F32)
    slot = lax.axis_index("ctx")
    core, row = slot % 2, slot // 2
    parts = values.reshape(2, 2, values.shape[0] // 4, values.shape[1])
    summed = pick(parts, core, 1).astype(F32) + swap(pick(parts, 1 - core, 1), 1).astype(F32)
    summed = summed.astype(BF16)
    return pick(summed, row, 0).astype(F32) + swap(pick(summed, 1 - row, 0), 2).astype(F32)


def scatter_sum(values, quads):
    if not quads:
        return lax.psum_scatter(values, BOTH, scatter_dimension=0, tiled=True).astype(F32)
    shard, ctx = lax.axis_index("shard"), lax.axis_index("ctx")
    core, row, column, layer = ctx % 2, ctx // 2, shard % 2, shard // 2
    layers = lax.axis_size("shard") // 2
    rows = values.shape[0] // (layers * 8)
    half = values.shape[1] // 2 // LANES * LANES
    parts = values.reshape(layers, 2, 2, 2, rows, values.shape[1])
    chip = pick(parts, core, 3).astype(F32) + swap(pick(parts, 1 - core, 3), 1).astype(F32)
    chip = chip.astype(BF16)
    left, right = chip[..., :half], chip[..., half:]
    left_in, right_in = swap(pick(left, 1 - column, 1), 4), swap(pick(right, 1 - row, 2), 2)
    left = (pick(left, column, 1).astype(F32) + left_in.astype(F32)).astype(BF16)
    right = (pick(right, row, 2).astype(F32) + right_in.astype(F32)).astype(BF16)
    left_in, right_in = swap(pick(left, 1 - row, 1), 2), swap(pick(right, 1 - column, 1), 4)
    left = pick(left, row, 1).astype(F32) + left_in.astype(F32)
    right = pick(right, column, 1).astype(F32) + right_in.astype(F32)
    plane = jnp.concatenate((left, right), axis=-1).astype(BF16)
    total = pick(plane, layer, 0).astype(F32)
    for step in range(1, layers):
        total = total + swap(pick(plane, layer ^ step, 0), 8 * step).astype(F32)
    return total


def small_sum(values, quads):
    if not quads:
        return lax.psum(values, BOTH)
    for mask in (1, 2, 4):
        values = values + swap(values, mask)
    arrived = [swap(values, 8 * step) for step in range(1, lax.axis_size("shard") // 2)]
    layer = lax.axis_index("shard") // 2
    stacked = jnp.stack([values] + arrived)
    return sum(pick(stacked, layer ^ step, 0) for step in range(stacked.shape[0]))


def fold(values, rows, columns):
    lead = values.shape[:-2]
    tall, wide = values.shape[-2] // 8, rows // 8
    step = values.shape[-1] // wide
    cut = values.reshape(lead + (tall, 8, values.shape[-1]))
    bands = []
    for band in range(wide):
        bands.append(
            jnp.concatenate(
                [cut[..., t, :, band * step : (band + 1) * step] for t in range(tall)], axis=-1
            )
        )
    return jnp.concatenate(bands, axis=-2)


def unfold(values, rows, columns):
    tall, wide = rows // 8, values.shape[-2] // 8
    step = columns // wide
    out = []
    for t in range(tall):
        out.append(
            jnp.concatenate(
                [
                    values[..., w * 8 : (w + 1) * 8, t * step : (t + 1) * step]
                    for w in range(wide)
                ],
                axis=-1,
            )
        )
    return jnp.concatenate(out, axis=-2)


def head_mask(shape, head_size, head):
    lane = lax.broadcasted_iota(jnp.int32, shape, 1)
    return lane // head_size == head


def pad_keys(source, target, span_rows):
    spans = source.shape[0] // span_rows
    for b in range(spans):
        target[b * LANES : b * LANES + span_rows, :] = source[
            b * span_rows : (b + 1) * span_rows, :
        ]


def skew(values, right):
    width = values.shape[1]
    row = lax.broadcasted_iota(jnp.int32, values.shape, 0)
    for bit in range((values.shape[0] - 1).bit_length()):
        shift = 1 << bit
        moved = pltpu.roll(values, shift if right else width - shift, 1)
        values = jnp.where((row >> bit) & 1 == 1, moved, values)
    return values


def dot_rows(left, right):
    return lax.dot_general(left, right, (((1,), (1,)), ((), ())), preferred_element_type=F32)


def dot_columns(left, right):
    return lax.dot_general(left, right, (((0,), (0,)), ((), ())), preferred_element_type=F32)


def probabilities(scores):
    top = jnp.max(scores, axis=1, keepdims=True)
    raised = jnp.exp(scores - top)
    return raised * (1.0 / jnp.sum(raised, axis=1, keepdims=True))


def self_forward_kernel(
    kind_ref, q_ref, k_ref, v_ref, line_ref, p_ref, o_ref, kp, vp, tables, s_ref, *, span_rows, head_size
):
    @pl.when(pl.program_id(0) == 0)
    def _():
        kp[...] = jnp.zeros(kp.shape, kp.dtype)
        vp[...] = jnp.zeros(vp.shape, vp.dtype)

    pad_keys(k_ref, kp, span_rows)
    pad_keys(v_ref, vp, span_rows)
    pair = LANES // head_size
    spans = k_ref.shape[0] // span_rows
    query_spans = q_ref.shape[0] // span_rows
    inside = lax.broadcasted_iota(jnp.int32, (span_rows, LANES), 1) < span_rows
    out = jnp.zeros(o_ref.shape, F32)
    for h in range(pair):
        tables[0] = jnp.full((span_rows, LANES), MASKED, F32)
        for k in range(4):
            line = jnp.broadcast_to(
                line_ref[0, h * 4 + k : h * 4 + k + 1, :], (span_rows, 2 * LANES)
            )
            if k < 3:
                line = skew(line, True)
            tables[k + 1] = jnp.where(inside, line[:, :LANES], MASKED)
        q = jnp.where(head_mask(q_ref.shape, head_size, h), q_ref[...], jnp.zeros((), BF16))
        s_ref[...] = dot_rows(q, kp[...]) * (head_size**-0.5)
        for a in range(query_spans):
            for b in range(spans):
                rows, columns = pl.ds(a * span_rows, span_rows), pl.ds(b * LANES, LANES)
                s_ref[rows, columns] = s_ref[rows, columns] + tables[kind_ref[a * spans + b]]
        probs = probabilities(s_ref[...]).astype(BF16)
        p_ref[h] = probs
        v = jnp.where(head_mask(vp.shape, head_size, h), vp[...], jnp.zeros((), BF16))
        out = out + jnp.dot(probs, v, preferred_element_type=F32)
    o_ref[...] = out.astype(BF16)


def cross_forward_kernel(q_ref, k_ref, v_ref, p_ref, o_ref, *, head_size):
    out = jnp.zeros(o_ref.shape, F32)
    for h in range(LANES // head_size):
        q = jnp.where(head_mask(q_ref.shape, head_size, h), q_ref[...], jnp.zeros((), BF16))
        probs = probabilities(dot_rows(q, k_ref[...]) * (head_size**-0.5)).astype(BF16)
        p_ref[h] = probs
        v = jnp.where(head_mask(v_ref.shape, head_size, h), v_ref[...], jnp.zeros((), BF16))
        out = out + jnp.dot(probs, v, preferred_element_type=F32)
    o_ref[...] = out.astype(BF16)


def pair_backward(h, q_ref, do_ref, keys, values, p_ref, head_size):
    grads = jnp.where(head_mask(do_ref.shape, head_size, h), do_ref[...], jnp.zeros((), BF16))
    q = jnp.where(head_mask(q_ref.shape, head_size, h), q_ref[...], jnp.zeros((), BF16))
    probs_low = p_ref[h]
    probs = probs_low.astype(F32)
    grad_probs = dot_rows(grads, values)
    delta = jnp.sum(probs * grad_probs, axis=1, keepdims=True)
    grad_scores = (probs * (grad_probs - delta)).astype(BF16)
    k = jnp.where(head_mask(keys.shape, head_size, h), keys, jnp.zeros((), BF16))
    grad_q = jnp.dot(grad_scores, k, preferred_element_type=F32)
    return grad_scores, grad_q, dot_columns(grad_scores, q), dot_columns(probs_low, grads)


def self_backward_kernel(
    kind_ref,
    q_ref,
    do_ref,
    k_ref,
    v_ref,
    p_ref,
    dq_ref,
    dk_ref,
    dv_ref,
    line_ref,
    kp,
    vp,
    tables,
    s_ref,
    *,
    span_rows,
    head_size,
):
    @pl.when(pl.program_id(0) == 0)
    def _():
        kp[...] = jnp.zeros(kp.shape, kp.dtype)
        vp[...] = jnp.zeros(vp.shape, vp.dtype)

    pad_keys(k_ref, kp, span_rows)
    pad_keys(v_ref, vp, span_rows)
    pair = LANES // head_size
    spans = k_ref.shape[0] // span_rows
    query_spans = q_ref.shape[0] // span_rows
    scale = head_size**-0.5
    grad_q = jnp.zeros(dq_ref.shape, F32)
    grad_k = jnp.zeros(kp.shape, F32)
    grad_v = jnp.zeros(vp.shape, F32)
    blank = jnp.zeros((span_rows, LANES), F32)
    for h in range(pair):
        scores, part_q, part_k, part_v = pair_backward(
            h, q_ref, do_ref, kp[...], vp[...], p_ref, head_size
        )
        grad_q, grad_k, grad_v = grad_q + part_q, grad_k + part_k, grad_v + part_v
        s_ref[...] = scores.astype(F32)
        tables[...] = jnp.zeros(tables.shape, F32)
        for a in range(query_spans):
            for b in range(spans):
                kind = kind_ref[a * spans + b]
                rows, columns = pl.ds(a * span_rows, span_rows), pl.ds(b * LANES, LANES)
                tables[kind] = tables[kind] + s_ref[rows, columns]
        for k in range(4):
            block = jnp.concatenate((tables[k + 1], blank), axis=1)
            if k < 3:
                block = skew(block, False)
            line_ref[0, h * 4 + k : h * 4 + k + 1, :] = jnp.sum(block, axis=0, keepdims=True)
    dq_ref[...] = (grad_q * scale).astype(BF16)
    grad_k = (grad_k * scale).astype(BF16)
    grad_v = grad_v.astype(BF16)
    for b in range(spans):
        dk_ref[b * span_rows : (b + 1) * span_rows, :] = grad_k[b * LANES : b * LANES + span_rows]
        dv_ref[b * span_rows : (b + 1) * span_rows, :] = grad_v[b * LANES : b * LANES + span_rows]


def cross_backward_kernel(
    q_ref, do_ref, k_ref, v_ref, p_ref, dq_ref, dk_ref, dv_ref, *, head_size
):
    scale = head_size**-0.5
    grad_q = jnp.zeros(dq_ref.shape, F32)
    grad_k = jnp.zeros(dk_ref.shape, F32)
    grad_v = jnp.zeros(dv_ref.shape, F32)
    for h in range(LANES // head_size):
        _, part_q, part_k, part_v = pair_backward(
            h, q_ref, do_ref, k_ref[...], v_ref[...], p_ref, head_size
        )
        grad_q, grad_k, grad_v = grad_q + part_q, grad_k + part_k, grad_v + part_v
    dq_ref[...] = (grad_q * scale).astype(BF16)
    dk_ref[...] = (grad_k * scale).astype(BF16)
    dv_ref[...] = grad_v.astype(BF16)


PARAMS = pltpu.CompilerParams(vmem_limit_bytes=48 * 1024 * 1024)


def columns_of(rows, offset=0):
    return pl.BlockSpec((rows, LANES), lambda g, *_: (0, g + offset))


def probs_spec(pair, rows, keys):
    return pl.BlockSpec((pair, rows, keys), lambda g, *_: (g, 0, 0))


def lines_spec():
    return pl.BlockSpec((1, 8, 2 * LANES), lambda g, *_: (g, 0, 0))


def self_forward(kinds, queries, keys_values, lines, span_rows, head_size):
    rows, width = queries.shape
    key_rows = keys_values.shape[0]
    groups, pair = width // LANES, LANES // head_size
    padded = key_rows // span_rows * LANES
    return pl.pallas_call(
        functools.partial(self_forward_kernel, span_rows=span_rows, head_size=head_size),
        grid_spec=pltpu.PrefetchScalarGridSpec(
            num_scalar_prefetch=1,
            grid=(groups,),
            in_specs=[
                columns_of(rows),
                columns_of(key_rows),
                columns_of(key_rows, groups),
                lines_spec(),
            ],
            out_specs=[probs_spec(pair, rows, padded), columns_of(rows)],
            scratch_shapes=[
                pltpu.VMEM((padded, LANES), BF16),
                pltpu.VMEM((padded, LANES), BF16),
                pltpu.VMEM((5, span_rows, LANES), F32),
                pltpu.VMEM((rows, padded), F32),
            ],
        ),
        out_shape=[
            jax.ShapeDtypeStruct((groups * pair, rows, padded), BF16),
            jax.ShapeDtypeStruct((rows, width), BF16),
        ],
        compiler_params=PARAMS,
    )(kinds, queries, keys_values, keys_values, lines)


def self_backward(kinds, queries, grads, keys_values, probs, span_rows, head_size):
    rows, width = queries.shape
    key_rows = keys_values.shape[0]
    groups, pair = width // LANES, LANES // head_size
    padded = probs.shape[2]
    return pl.pallas_call(
        functools.partial(self_backward_kernel, span_rows=span_rows, head_size=head_size),
        grid_spec=pltpu.PrefetchScalarGridSpec(
            num_scalar_prefetch=1,
            grid=(groups,),
            in_specs=[
                columns_of(rows),
                columns_of(rows),
                columns_of(key_rows),
                columns_of(key_rows, groups),
                probs_spec(pair, rows, padded),
            ],
            out_specs=[
                columns_of(rows),
                columns_of(key_rows),
                columns_of(key_rows),
                lines_spec(),
            ],
            scratch_shapes=[
                pltpu.VMEM((padded, LANES), BF16),
                pltpu.VMEM((padded, LANES), BF16),
                pltpu.VMEM((5, span_rows, LANES), F32),
                pltpu.VMEM((rows, padded), F32),
            ],
        ),
        out_shape=[
            jax.ShapeDtypeStruct((rows, width), BF16),
            jax.ShapeDtypeStruct((key_rows, width), BF16),
            jax.ShapeDtypeStruct((key_rows, width), BF16),
            jax.ShapeDtypeStruct((groups, 8, 2 * LANES), F32),
        ],
        compiler_params=PARAMS,
    )(kinds, queries, grads, keys_values, keys_values, probs)


def cross_forward(queries, keys_values, head_size):
    rows, width = queries.shape
    key_rows = keys_values.shape[0]
    groups, pair = width // LANES, LANES // head_size
    return pl.pallas_call(
        functools.partial(cross_forward_kernel, head_size=head_size),
        grid=(groups,),
        in_specs=[columns_of(rows), columns_of(key_rows), columns_of(key_rows, groups)],
        out_specs=[probs_spec(pair, rows, key_rows), columns_of(rows)],
        out_shape=[
            jax.ShapeDtypeStruct((groups * pair, rows, key_rows), BF16),
            jax.ShapeDtypeStruct((rows, width), BF16),
        ],
        compiler_params=PARAMS,
    )(queries, keys_values, keys_values)


def cross_backward(queries, grads, keys_values, probs, head_size):
    rows, width = queries.shape
    key_rows = keys_values.shape[0]
    groups, pair = width // LANES, LANES // head_size
    return pl.pallas_call(
        functools.partial(cross_backward_kernel, head_size=head_size),
        grid=(groups,),
        in_specs=[
            columns_of(rows),
            columns_of(rows),
            columns_of(key_rows),
            columns_of(key_rows, groups),
            probs_spec(pair, rows, key_rows),
        ],
        out_specs=[columns_of(rows), columns_of(key_rows), columns_of(key_rows)],
        out_shape=[
            jax.ShapeDtypeStruct((rows, width), BF16),
            jax.ShapeDtypeStruct((key_rows, width), BF16),
            jax.ShapeDtypeStruct((key_rows, width), BF16),
        ],
        compiler_params=PARAMS,
    )(queries, grads, keys_values, keys_values, probs)


def line_buckets(buckets, span_rows, table_rows):
    place = jnp.arange(2 * LANES, dtype=jnp.int32)
    place = jnp.where(place < LANES, place, place - 2 * LANES)
    distance = jnp.arange(3, dtype=jnp.int32)[:, None] * span_rows - place[None, :]
    known = buckets.shape[0]
    hits = distance[:, :, None] == jnp.arange(known, dtype=jnp.int32)
    bucket = jnp.sum(jnp.where(hits, buckets, 0), axis=-1)
    bucket = jnp.where(distance >= known, table_rows - 1, bucket)
    onehot = bucket[:, :, None] == jnp.arange(table_rows, dtype=jnp.int32)
    return (onehot & (distance >= 0)[:, :, None]).astype(F32), distance >= 0


def bias_lines(table, onehot, valid, pair):
    heads = table.shape[1]
    lines = jnp.einsum("kmb,bh->hkm", onehot, table, precision=PRECISE)
    lines = jnp.where(valid[None], lines, MASKED)
    last = jnp.broadcast_to(table[-1][:, None, None], (heads, 1, lines.shape[2]))
    lines = jnp.concatenate((lines, last), axis=1)
    return lines.reshape(heads // pair, pair * 4, lines.shape[2])


def table_gradient(lines, onehot, heads):
    lines = lines.reshape(heads, 4, lines.shape[2])
    grads = jnp.einsum("hkm,kmb->bh", lines[:, :3], onehot, precision=PRECISE)
    return grads.at[-1].add(jnp.sum(lines[:, 3], axis=-1))


def block_kinds(span_order, first_span, query_spans):
    own = lax.dynamic_slice_in_dim(span_order, first_span, query_spans, 0)
    apart = own[:, None] - span_order[None, :]
    kinds = jnp.where(apart < 0, 0, jnp.where(apart > 2, 4, apart + 1))
    return kinds.reshape(-1).astype(jnp.int32)


def per_device(
    inputs,
    encoder_states,
    cotangent,
    span_order,
    buckets,
    gain_self,
    self_query,
    self_key,
    self_value,
    self_out,
    gain_cross,
    cross_query,
    cross_key,
    cross_value,
    cross_out,
    gain_feed,
    feed_gate,
    feed_up,
    feed_down,
    bias_table,
):
    shards, slots = lax.axis_size("shard"), lax.axis_size("ctx")
    shard_rows, width = self_query.shape
    down_rows = feed_down.shape[0]
    feed = feed_gate.shape[1]
    quads = slots == 4 and shards in (2, 4, 8) and shard_rows % 8 == 0 and down_rows % 8 == 0
    token_rows = inputs.shape[1]
    heads = bias_table.shape[1]
    head_size = width // heads
    pair = LANES // head_size
    table_rows = bias_table.shape[0]
    span_rows = token_rows // 2
    slot = lax.axis_index("ctx")
    enc_rows = encoder_states.shape[1]

    gains = jnp.stack((gain_self, gain_cross, gain_feed), axis=1)
    gains = jnp.pad(gains, ((0, 0), (0, LANES - gains.shape[1])))
    mine = [
        self_query,
        self_key,
        self_value,
        self_out,
        cross_query,
        cross_key,
        cross_value,
        cross_out,
        feed_gate,
        feed_up,
        gains,
    ]
    if quads:
        mine.append(fold(feed_down, shard_rows, feed_down.size // shard_rows))
    packed = lax.all_gather(jnp.concatenate(mine, axis=1), BOTH, axis=0, tiled=True)

    def columns(first, last):
        return lax.slice_in_dim(packed, first, last, axis=1)

    w_query, w_key_value = columns(0, width), columns(width, 3 * width)
    w_out, w_cross_query = columns(3 * width, 4 * width), columns(4 * width, 5 * width)
    w_cross_key_value, w_cross_out = columns(5 * width, 7 * width), columns(7 * width, 8 * width)
    base = 8 * width
    w_gate, w_up = columns(base, base + feed), columns(base + feed, base + 2 * feed)
    base = base + 2 * feed
    gain_rows = columns(base, base + LANES).T.astype(F32)
    g_self, g_cross, g_feed = gain_rows[0], gain_rows[1], gain_rows[2]
    if quads:
        folded = columns(base + LANES, packed.shape[1])
        folded = folded.reshape(shards * slots, shard_rows, folded.shape[1])
        w_down = unfold(folded, down_rows, width).reshape(feed, width)
    else:
        w_down = lax.all_gather(feed_down, BOTH, axis=0, tiled=True)

    sequence = ctx_gather(jnp.concatenate((inputs[0], encoder_states[0]), axis=0), quads)
    sequence = sequence.reshape(slots, token_rows + enc_rows, width)
    tokens_all = sequence[:, :token_rows].reshape(slots * token_rows, width).astype(F32)
    encoded = sequence[:, token_rows:].reshape(slots * enc_rows, width)

    onehot, valid = line_buckets(buckets, span_rows, table_rows)
    lines = bias_lines(bias_table, onehot, valid, pair)
    kinds = block_kinds(span_order, slot * 2, 2)

    tokens = inputs[0].astype(F32)
    unit_all = tokens_all * inverse_norm(tokens_all)
    normed_all = (unit_all * g_self).astype(BF16)
    inverse_self = inverse_norm(tokens)
    unit_self = tokens * inverse_self
    normed_self = (unit_self * g_self).astype(BF16)
    queries = project(normed_self, w_query).astype(BF16)
    keys_values = project(normed_all, w_key_value).astype(BF16)
    probs, attended = self_forward(kinds, queries, keys_values, lines, span_rows, head_size)
    after_self = tokens + project(attended, w_out)
    inverse_cross = inverse_norm(after_self)
    unit_cross = after_self * inverse_cross
    normed_cross = (unit_cross * g_cross).astype(BF16)
    cross_q = project(normed_cross, w_cross_query).astype(BF16)
    cross_kv = project(encoded, w_cross_key_value).astype(BF16)
    cross_probs, cross_att = cross_forward(cross_q, cross_kv, head_size)
    after_cross = after_self + project(cross_att, w_cross_out)
    inverse_feed = inverse_norm(after_cross)
    unit_feed = after_cross * inverse_feed
    normed_feed = (unit_feed * g_feed).astype(BF16)
    gate_pre = project(normed_feed, w_gate)
    up_pre = project(normed_feed, w_up)
    gated, gated_pull = jax.vjp(
        lambda first, second: jax.nn.gelu(first, approximate=True) * second, gate_pre, up_pre
    )
    hidden = gated.astype(BF16)
    outputs = (after_cross + project(hidden, w_down)).astype(BF16)

    grad_out = cotangent[0]
    outer = grad_out.astype(F32)
    grad_gate, grad_up = gated_pull(project_back(grad_out, w_down))
    grad_gate, grad_up = grad_gate.astype(BF16), grad_up.astype(BF16)
    down_grad = outer_sum(hidden, grad_out).astype(BF16)
    feed_grads = [
        outer_sum(normed_feed, grad_gate).astype(BF16),
        outer_sum(normed_feed, grad_up).astype(BF16),
    ]
    if quads:
        folded = down_grad.reshape(shards * slots, down_rows, width)
        folded = fold(folded, shard_rows, down_rows * width // shard_rows)
        feed_grads.append(folded.reshape(shards * slots * shard_rows, folded.shape[2]))
    own_feed = scatter_sum(jnp.concatenate(feed_grads, axis=1), quads)
    own_gate, own_up = own_feed[:, :feed], own_feed[:, feed : 2 * feed]
    if quads:
        own_down = unfold(own_feed[:, 2 * feed :], down_rows, width)
    else:
        own_down = scatter_sum(down_grad, quads)
    grad_normed = project_back(grad_gate, w_gate) + project_back(grad_up, w_up)
    gain_feed_grad = jnp.sum(grad_normed * unit_feed, axis=0)
    grad_cross_out = outer + norm_back(after_cross, inverse_feed, g_feed, grad_normed)

    grad_low = grad_cross_out.astype(BF16)
    cross_out_grad = outer_sum(cross_att, grad_low).astype(BF16)
    grad_att = project_back(grad_low, w_cross_out).astype(BF16)
    grad_cq, part_ck, part_cv = cross_backward(cross_q, grad_att, cross_kv, cross_probs, head_size)
    cross_query_grad = outer_sum(normed_cross, grad_cq).astype(BF16)
    part_ckv = jnp.concatenate((part_ck, part_cv), axis=1)
    cross_kv_grad = outer_sum(encoded, part_ckv).astype(BF16)
    encoder_grad = ctx_scatter_sum(project_back(part_ckv, w_cross_key_value).astype(BF16), quads)
    grad_normed = project_back(grad_cq, w_cross_query)
    gain_cross_grad = jnp.sum(grad_normed * unit_cross, axis=0)
    grad_self_out = grad_cross_out + norm_back(after_self, inverse_cross, g_cross, grad_normed)

    grad_low = grad_self_out.astype(BF16)
    self_out_grad = outer_sum(attended, grad_low).astype(BF16)
    grad_att = project_back(grad_low, w_out).astype(BF16)
    grad_q, part_k, part_v, grad_lines = self_backward(
        kinds, queries, grad_att, keys_values, probs, span_rows, head_size
    )
    query_grad = outer_sum(normed_self, grad_q).astype(BF16)
    part_kv = jnp.concatenate((part_k, part_v), axis=1)
    kv_grad = outer_sum(normed_all, part_kv).astype(BF16)
    own = scatter_sum(
        jnp.concatenate(
            (query_grad, kv_grad, self_out_grad, cross_query_grad, cross_kv_grad, cross_out_grad),
            axis=1,
        ),
        quads,
    )
    own = [own[:, i * width : (i + 1) * width] for i in range(8)]
    grad_kv_normed = project_back(part_kv, w_key_value)
    grad_q_normed = project_back(grad_q, w_query)
    gain_self_grad = jnp.sum(grad_kv_normed * unit_all, axis=0) + jnp.sum(
        grad_q_normed * unit_self, axis=0
    )
    grad_normed = grad_q_normed + ctx_scatter_sum(grad_kv_normed.astype(BF16), quads)
    input_grad = grad_self_out + norm_back(tokens, inverse_self, g_self, grad_normed)

    table_part = table_gradient(grad_lines, onehot, heads)
    small = jnp.concatenate(
        (gain_self_grad, gain_cross_grad, gain_feed_grad, table_part.reshape(-1))
    )
    tile = 8 * LANES
    extent = small.shape[0]
    small = jnp.pad(small, (0, -extent % tile)).reshape(-1, LANES)
    small = small_sum(small, quads).reshape(-1)
    position = lax.axis_index(BOTH) * shard_rows
    own_gains = [
        lax.dynamic_slice_in_dim(small, i * width + position, shard_rows, 0) for i in range(3)
    ]
    table_total = small[3 * width : extent].reshape(table_rows, heads)
    return (
        outputs[None],
        input_grad.astype(BF16)[None],
        encoder_grad.astype(BF16)[None],
        own_gains[0],
        own[0],
        own[1],
        own[2],
        own[3],
        own_gains[1],
        own[4],
        own[5],
        own[6],
        own[7],
        own_gains[2],
        own_gate,
        own_up,
        own_down,
        table_total,
    )


def solution(mesh):
    in_specs = (
        P("shard", "ctx", None),
        P("shard", "ctx", None),
        P("shard", "ctx", None),
        P(),
        P(),
        P(("shard", "ctx")),
        P(("shard", "ctx"), None),
        P(("shard", "ctx"), None),
        P(("shard", "ctx"), None),
        P(("shard", "ctx"), None),
        P(("shard", "ctx")),
        P(("shard", "ctx"), None),
        P(("shard", "ctx"), None),
        P(("shard", "ctx"), None),
        P(("shard", "ctx"), None),
        P(("shard", "ctx")),
        P(("shard", "ctx"), None),
        P(("shard", "ctx"), None),
        P(("shard", "ctx"), None),
        P(),
    )
    out_specs = (
        P("shard", "ctx", None),
        P("shard", "ctx", None),
        P("shard", "ctx", None),
        P(("shard", "ctx")),
        P(("shard", "ctx"), None),
        P(("shard", "ctx"), None),
        P(("shard", "ctx"), None),
        P(("shard", "ctx"), None),
        P(("shard", "ctx")),
        P(("shard", "ctx"), None),
        P(("shard", "ctx"), None),
        P(("shard", "ctx"), None),
        P(("shard", "ctx"), None),
        P(("shard", "ctx")),
        P(("shard", "ctx"), None),
        P(("shard", "ctx"), None),
        P(("shard", "ctx"), None),
        P(),
    )
    return jax.shard_map(
        per_device, mesh=mesh, in_specs=in_specs, out_specs=out_specs, check_vma=False
    )
```

```python
import functools

import jax
import jax.numpy as jnp
from jax import lax
from jax.experimental import pallas as pl
from jax.experimental.pallas import tpu as pltpu
from jax.sharding import PartitionSpec as P

EPSILON = 1e-06
MASKED = -1e30
PRECISE = lax.Precision.HIGHEST
LANES = 128
BOTH = ("shard", "ctx")
F32 = jnp.float32
BF16 = jnp.bfloat16


def inverse_norm(values):
    return lax.rsqrt(jnp.mean(values * values, axis=-1, keepdims=True) + EPSILON)


def norm_back(values, inverse, gain, grads):
    weighted = gain * grads
    middle = jnp.mean(weighted * values, axis=-1, keepdims=True)
    return inverse * weighted - values * (inverse * inverse * inverse) * middle


def project(left, right):
    return jnp.dot(left, right, preferred_element_type=F32)


def project_back(grads, weight):
    return lax.dot_general(grads, weight, (((1,), (1,)), ((), ())), preferred_element_type=F32)


def outer_sum(left, grads):
    return lax.dot_general(left, grads, (((0,), (0,)), ((), ())), preferred_element_type=F32)


def swap(values, mask):
    count = lax.axis_size("shard") * lax.axis_size("ctx")
    return lax.ppermute(values, BOTH, [(i, i ^ mask) for i in range(count)])


def pick(values, index, axis):
    return lax.dynamic_index_in_dim(values, index, axis, keepdims=False)


def paired(first, second, flag):
    joined = jnp.concatenate((first, second), axis=0)
    return jnp.where(flag == 0, joined, jnp.concatenate((second, first), axis=0))


def ctx_gather(values, quads):
    if not quads:
        return lax.all_gather(values, "ctx", axis=0, tiled=True)
    slot = lax.axis_index("ctx")
    far = swap(values, 2)
    near = paired(values, swap(values, 1), slot % 2)
    far = paired(far, swap(far, 1), slot % 2)
    return paired(near, far, slot // 2)


def ctx_scatter_sum(values, quads):
    if not quads:
        return lax.psum_scatter(values, "ctx", scatter_dimension=0, tiled=True).astype(F32)
    slot = lax.axis_index("ctx")
    core, row = slot % 2, slot // 2
    parts = values.reshape(2, 2, values.shape[0] // 4, values.shape[1])
    summed = pick(parts, core, 1).astype(F32) + swap(pick(parts, 1 - core, 1), 1).astype(F32)
    summed = summed.astype(BF16)
    return pick(summed, row, 0).astype(F32) + swap(pick(summed, 1 - row, 0), 2).astype(F32)


def place():
    shard, ctx = lax.axis_index("shard"), lax.axis_index("ctx")
    return ctx % 2, ctx // 2, shard % 2, shard // 2


def add_low(first, second):
    return (first.astype(F32) + second.astype(F32)).astype(BF16)


def by_chip(values):
    layers = lax.axis_size("shard") // 2
    return values.reshape(layers, 2, 2, values.shape[0] // (layers * 4), values.shape[1])


def plane_sends(left, right):
    _, row, column, _ = place()
    left, right = by_chip(left), by_chip(right)
    sends = pick(left, 1 - column, 1), pick(right, 1 - row, 2)
    return sends + (pick(left, column, 1), pick(right, row, 2))


def plane_first(left_out, right_out):
    return swap(left_out, 4), swap(right_out, 2)


def plane_second_sends(left, left_in, right, right_in):
    _, row, column, _ = place()
    left, right = add_low(left, left_in), add_low(right, right_in)
    sends = pick(left, 1 - row, 1), pick(right, 1 - column, 1)
    return sends + (pick(left, row, 1), pick(right, column, 1))


def plane_second(left_out, right_out):
    return swap(left_out, 2), swap(right_out, 4)


def plane_sum(left, left_in, right, right_in):
    return jnp.concatenate((add_low(left, left_in), add_low(right, right_in)), axis=-1)


def z_sends(plane):
    layer = lax.axis_index("shard") // 2
    return [pick(plane, layer ^ step, 0) for step in range(plane.shape[0])]


def z_swaps(parts):
    return [swap(part, 8 * step) for step, part in enumerate(parts) if step]


def z_total(own, arrived):
    total = own.astype(F32)
    for part in arrived:
        total = total + part.astype(F32)
    return total


def between_cores(total):
    core = lax.axis_index("ctx") % 2
    total = total.reshape(2, total.shape[0] // 2, total.shape[1])
    own = pick(total, core, 0)
    other = swap(pick(total, 1 - core, 0).astype(BF16), 1).astype(F32)
    return jnp.where(core == 0, own, other), jnp.where(core == 0, other, own)


def core_halves(values):
    core = lax.axis_index("ctx") % 2
    half = values.shape[1] // 2
    low, high = values[:, :half], values[:, half:]
    return jnp.where(core == 0, low, high), jnp.where(core == 0, high, low)


def tied(value, *others):
    return lax.optimization_barrier((value,) + others)


def scatter_sum(values):
    return lax.psum_scatter(values, BOTH, scatter_dimension=0, tiled=True).astype(F32)


def small_plane_sum(values):
    for mask in (1, 2, 4):
        values = values + swap(values, mask)
    return values


def small_z_sum(values):
    arrived = [swap(values, 8 * step) for step in range(1, lax.axis_size("shard") // 2)]
    layer = lax.axis_index("shard") // 2
    stacked = jnp.stack([values] + arrived)
    return sum(pick(stacked, layer ^ step, 0) for step in range(stacked.shape[0]))


def fold(values, rows, columns):
    lead = values.shape[:-2]
    tall, wide = values.shape[-2] // 8, rows // 8
    step = values.shape[-1] // wide
    cut = values.reshape(lead + (tall, 8, values.shape[-1]))
    bands = []
    for band in range(wide):
        bands.append(
            jnp.concatenate(
                [cut[..., t, :, band * step : (band + 1) * step] for t in range(tall)], axis=-1
            )
        )
    return jnp.concatenate(bands, axis=-2)


def unfold(values, rows, columns):
    tall, wide = rows // 8, values.shape[-2] // 8
    step = columns // wide
    out = []
    for t in range(tall):
        out.append(
            jnp.concatenate(
                [
                    values[..., w * 8 : (w + 1) * 8, t * step : (t + 1) * step]
                    for w in range(wide)
                ],
                axis=-1,
            )
        )
    return jnp.concatenate(out, axis=-2)


def head_mask(shape, head_size, head):
    lane = lax.broadcasted_iota(jnp.int32, shape, 1)
    return lane // head_size == head


def pad_keys(source, target, span_rows):
    spans = source.shape[0] // span_rows
    for b in range(spans):
        target[b * LANES : b * LANES + span_rows, :] = source[
            b * span_rows : (b + 1) * span_rows, :
        ]


def skew(values, right):
    width = values.shape[1]
    row = lax.broadcasted_iota(jnp.int32, values.shape, 0)
    for bit in range((values.shape[0] - 1).bit_length()):
        shift = 1 << bit
        moved = pltpu.roll(values, shift if right else width - shift, 1)
        values = jnp.where((row >> bit) & 1 == 1, moved, values)
    return values


def dot_rows(left, right):
    return lax.dot_general(left, right, (((1,), (1,)), ((), ())), preferred_element_type=F32)


def dot_columns(left, right):
    return lax.dot_general(left, right, (((0,), (0,)), ((), ())), preferred_element_type=F32)


def probabilities(scores):
    top = jnp.max(scores, axis=1, keepdims=True)
    raised = jnp.exp(scores - top)
    return raised * (1.0 / jnp.sum(raised, axis=1, keepdims=True))


def self_forward_kernel(
    kind_ref, q_ref, k_ref, v_ref, line_ref, p_ref, o_ref, kp, vp, tables, s_ref, *, span_rows, head_size
):
    @pl.when(pl.program_id(0) == 0)
    def _():
        kp[...] = jnp.zeros(kp.shape, kp.dtype)
        vp[...] = jnp.zeros(vp.shape, vp.dtype)

    pad_keys(k_ref, kp, span_rows)
    pad_keys(v_ref, vp, span_rows)
    pair = LANES // head_size
    spans = k_ref.shape[0] // span_rows
    query_spans = q_ref.shape[0] // span_rows
    inside = lax.broadcasted_iota(jnp.int32, (span_rows, LANES), 1) < span_rows
    out = jnp.zeros(o_ref.shape, F32)
    for h in range(pair):
        tables[0] = jnp.full((span_rows, LANES), MASKED, F32)
        for k in range(4):
            line = jnp.broadcast_to(
                line_ref[0, h * 4 + k : h * 4 + k + 1, :], (span_rows, 2 * LANES)
            )
            if k < 3:
                line = skew(line, True)
            tables[k + 1] = jnp.where(inside, line[:, :LANES], MASKED)
        q = jnp.where(head_mask(q_ref.shape, head_size, h), q_ref[...], jnp.zeros((), BF16))
        s_ref[...] = dot_rows(q, kp[...]) * (head_size**-0.5)
        for a in range(query_spans):
            for b in range(spans):
                rows, columns = pl.ds(a * span_rows, span_rows), pl.ds(b * LANES, LANES)
                s_ref[rows, columns] = s_ref[rows, columns] + tables[kind_ref[a * spans + b]]
        probs = probabilities(s_ref[...]).astype(BF16)
        p_ref[h] = probs
        v = jnp.where(head_mask(vp.shape, head_size, h), vp[...], jnp.zeros((), BF16))
        out = out + jnp.dot(probs, v, preferred_element_type=F32)
    o_ref[...] = out.astype(BF16)


def cross_forward_kernel(q_ref, k_ref, v_ref, p_ref, o_ref, *, head_size):
    out = jnp.zeros(o_ref.shape, F32)
    for h in range(LANES // head_size):
        q = jnp.where(head_mask(q_ref.shape, head_size, h), q_ref[...], jnp.zeros((), BF16))
        probs = probabilities(dot_rows(q, k_ref[...]) * (head_size**-0.5)).astype(BF16)
        p_ref[h] = probs
        v = jnp.where(head_mask(v_ref.shape, head_size, h), v_ref[...], jnp.zeros((), BF16))
        out = out + jnp.dot(probs, v, preferred_element_type=F32)
    o_ref[...] = out.astype(BF16)


def pair_backward(h, q_ref, do_ref, keys, values, p_ref, head_size):
    grads = jnp.where(head_mask(do_ref.shape, head_size, h), do_ref[...], jnp.zeros((), BF16))
    q = jnp.where(head_mask(q_ref.shape, head_size, h), q_ref[...], jnp.zeros((), BF16))
    probs_low = p_ref[h]
    probs = probs_low.astype(F32)
    grad_probs = dot_rows(grads, values)
    delta = jnp.sum(probs * grad_probs, axis=1, keepdims=True)
    grad_scores = (probs * (grad_probs - delta)).astype(BF16)
    k = jnp.where(head_mask(keys.shape, head_size, h), keys, jnp.zeros((), BF16))
    grad_q = jnp.dot(grad_scores, k, preferred_element_type=F32)
    return grad_scores, grad_q, dot_columns(grad_scores, q), dot_columns(probs_low, grads)


def self_backward_kernel(
    kind_ref,
    q_ref,
    do_ref,
    k_ref,
    v_ref,
    p_ref,
    dq_ref,
    dkv_ref,
    line_ref,
    kp,
    vp,
    tables,
    s_ref,
    *,
    span_rows,
    head_size,
):
    @pl.when(pl.program_id(0) == 0)
    def _():
        kp[...] = jnp.zeros(kp.shape, kp.dtype)
        vp[...] = jnp.zeros(vp.shape, vp.dtype)

    pad_keys(k_ref, kp, span_rows)
    pad_keys(v_ref, vp, span_rows)
    pair = LANES // head_size
    spans = k_ref.shape[0] // span_rows
    query_spans = q_ref.shape[0] // span_rows
    scale = head_size**-0.5
    grad_q = jnp.zeros(dq_ref.shape, F32)
    grad_k = jnp.zeros(kp.shape, F32)
    grad_v = jnp.zeros(vp.shape, F32)
    blank = jnp.zeros((span_rows, LANES), F32)
    for h in range(pair):
        scores, part_q, part_k, part_v = pair_backward(
            h, q_ref, do_ref, kp[...], vp[...], p_ref, head_size
        )
        grad_q, grad_k, grad_v = grad_q + part_q, grad_k + part_k, grad_v + part_v
        s_ref[...] = scores.astype(F32)
        tables[...] = jnp.zeros(tables.shape, F32)
        for a in range(query_spans):
            for b in range(spans):
                kind = kind_ref[a * spans + b]
                rows, columns = pl.ds(a * span_rows, span_rows), pl.ds(b * LANES, LANES)
                tables[kind] = tables[kind] + s_ref[rows, columns]
        for k in range(4):
            block = jnp.concatenate((tables[k + 1], blank), axis=1)
            if k < 3:
                block = skew(block, False)
            line_ref[0, h * 4 + k : h * 4 + k + 1, :] = jnp.sum(block, axis=0, keepdims=True)
    dq_ref[...] = (grad_q * scale).astype(BF16)
    grad_k = (grad_k * scale).astype(BF16)
    grad_v = grad_v.astype(BF16)
    for b in range(spans):
        target, source = pl.ds(b * span_rows, span_rows), slice(b * LANES, b * LANES + span_rows)
        dkv_ref[0, target, :] = grad_k[source]
        dkv_ref[1, target, :] = grad_v[source]


def cross_backward_kernel(
    _, q_ref, do_ref, k_ref, v_ref, p_ref, dq_ref, dkv_ref, *, head_size
):
    scale = head_size**-0.5
    grad_q = jnp.zeros(dq_ref.shape, F32)
    grad_k = jnp.zeros(k_ref.shape, F32)
    grad_v = jnp.zeros(v_ref.shape, F32)
    for h in range(LANES // head_size):
        _, part_q, part_k, part_v = pair_backward(
            h, q_ref, do_ref, k_ref[...], v_ref[...], p_ref, head_size
        )
        grad_q, grad_k, grad_v = grad_q + part_q, grad_k + part_k, grad_v + part_v
    dq_ref[...] = (grad_q * scale).astype(BF16)
    dkv_ref[0] = (grad_k * scale).astype(BF16)
    dkv_ref[1] = grad_v.astype(BF16)


PARAMS = pltpu.CompilerParams(vmem_limit_bytes=48 * 1024 * 1024)


def columns_of(rows, offset=0):
    return pl.BlockSpec((rows, LANES), lambda g, *_: (0, g + offset))


def probs_spec(pair, rows, keys):
    return pl.BlockSpec((pair, rows, keys), lambda g, *_: (g, 0, 0))


def lines_spec():
    return pl.BlockSpec((1, 8, 2 * LANES), lambda g, *_: (g, 0, 0))


def self_forward(kinds, queries, keys_values, lines, span_rows, head_size):
    rows, width = queries.shape
    key_rows = keys_values.shape[0]
    groups, pair = width // LANES, LANES // head_size
    padded = key_rows // span_rows * LANES
    return pl.pallas_call(
        functools.partial(self_forward_kernel, span_rows=span_rows, head_size=head_size),
        grid_spec=pltpu.PrefetchScalarGridSpec(
            num_scalar_prefetch=1,
            grid=(groups,),
            in_specs=[
                columns_of(rows),
                columns_of(key_rows),
                columns_of(key_rows, groups),
                lines_spec(),
            ],
            out_specs=[probs_spec(pair, rows, padded), columns_of(rows)],
            scratch_shapes=[
                pltpu.VMEM((padded, LANES), BF16),
                pltpu.VMEM((padded, LANES), BF16),
                pltpu.VMEM((5, span_rows, LANES), F32),
                pltpu.VMEM((rows, padded), F32),
            ],
        ),
        out_shape=[
            jax.ShapeDtypeStruct((groups * pair, rows, padded), BF16),
            jax.ShapeDtypeStruct((rows, width), BF16),
        ],
        compiler_params=PARAMS,
    )(kinds, queries, keys_values, keys_values, lines)


def backward_specs(rows, key_rows, padded, groups, pair):
    def at(offset=0):
        return lambda g, scalars: (0, g + scalars[scalars.shape[0] - 1] + offset)

    ins = [
        pl.BlockSpec((rows, LANES), at()),
        pl.BlockSpec((rows, LANES), at()),
        pl.BlockSpec((key_rows, LANES), at()),
        pl.BlockSpec((key_rows, LANES), at(groups)),
        pl.BlockSpec(
            (pair, rows, padded), lambda g, scalars: (g + scalars[scalars.shape[0] - 1], 0, 0)
        ),
    ]
    outs = [
        pl.BlockSpec((rows, LANES), lambda g, _: (0, g)),
        pl.BlockSpec((2, key_rows, LANES), lambda g, _: (0, 0, g)),
    ]
    return ins, outs


def self_backward(scalars, count, queries, grads, keys_values, probs, span_rows, head_size):
    rows, width = queries.shape
    key_rows = keys_values.shape[0]
    groups, pair = width // LANES, LANES // head_size
    padded = probs.shape[2]
    in_specs, out_specs = backward_specs(rows, key_rows, padded, groups, pair)
    return pl.pallas_call(
        functools.partial(self_backward_kernel, span_rows=span_rows, head_size=head_size),
        grid_spec=pltpu.PrefetchScalarGridSpec(
            num_scalar_prefetch=1,
            grid=(count,),
            in_specs=in_specs,
            out_specs=out_specs + [lines_spec()],
            scratch_shapes=[
                pltpu.VMEM((padded, LANES), BF16),
                pltpu.VMEM((padded, LANES), BF16),
                pltpu.VMEM((5, span_rows, LANES), F32),
                pltpu.VMEM((rows, padded), F32),
            ],
        ),
        out_shape=[
            jax.ShapeDtypeStruct((rows, count * LANES), BF16),
            jax.ShapeDtypeStruct((2, key_rows, count * LANES), BF16),
            jax.ShapeDtypeStruct((count, 8, 2 * LANES), F32),
        ],
        compiler_params=PARAMS,
    )(scalars, queries, grads, keys_values, keys_values, probs)


def cross_backward(scalars, count, queries, grads, keys_values, probs, head_size):
    rows, width = queries.shape
    key_rows = keys_values.shape[0]
    groups, pair = width // LANES, LANES // head_size
    in_specs, out_specs = backward_specs(rows, key_rows, key_rows, groups, pair)
    return pl.pallas_call(
        functools.partial(cross_backward_kernel, head_size=head_size),
        grid_spec=pltpu.PrefetchScalarGridSpec(
            num_scalar_prefetch=1, grid=(count,), in_specs=in_specs, out_specs=out_specs
        ),
        out_shape=[
            jax.ShapeDtypeStruct((rows, count * LANES), BF16),
            jax.ShapeDtypeStruct((2, key_rows, count * LANES), BF16),
        ],
        compiler_params=PARAMS,
    )(scalars, queries, grads, keys_values, keys_values, probs)


def cross_forward(queries, keys_values, head_size):
    rows, width = queries.shape
    key_rows = keys_values.shape[0]
    groups, pair = width // LANES, LANES // head_size
    return pl.pallas_call(
        functools.partial(cross_forward_kernel, head_size=head_size),
        grid=(groups,),
        in_specs=[columns_of(rows), columns_of(key_rows), columns_of(key_rows, groups)],
        out_specs=[probs_spec(pair, rows, key_rows), columns_of(rows)],
        out_shape=[
            jax.ShapeDtypeStruct((groups * pair, rows, key_rows), BF16),
            jax.ShapeDtypeStruct((rows, width), BF16),
        ],
        compiler_params=PARAMS,
    )(queries, keys_values, keys_values)


def pack_kernel(*refs, shard_rows):
    *parts, down, out = refs
    pieces = [part[...].astype(F32) for part in parts]
    moved = down[...].astype(F32)
    pieces.append(fold(moved, shard_rows, moved.size // shard_rows))
    out[...] = jnp.concatenate(pieces, axis=1).astype(out.dtype)


def pack_weights(parts, down, shard_rows):
    columns = sum(part.shape[1] for part in parts) + down.size // shard_rows
    return pl.pallas_call(
        functools.partial(pack_kernel, shard_rows=shard_rows),
        out_shape=jax.ShapeDtypeStruct((shard_rows, columns), down.dtype),
        compiler_params=PARAMS,
    )(*parts, down)


def move_kernel(in_ref, out_ref, *, folding):
    move = fold if folding else unfold
    for i in range(in_ref.shape[0]):
        moved = move(in_ref[i].astype(F32), out_ref.shape[1], out_ref.shape[2])
        out_ref[i] = moved.astype(out_ref.dtype)


def move_tiles(values, rows, columns, folding):
    blocks = values.shape[0]
    step = 8 if blocks % 8 == 0 else 1
    return pl.pallas_call(
        functools.partial(move_kernel, folding=folding),
        grid=(blocks // step,),
        in_specs=[pl.BlockSpec((step,) + values.shape[1:], lambda g: (g, 0, 0))],
        out_specs=pl.BlockSpec((step, rows, columns), lambda g: (g, 0, 0)),
        out_shape=jax.ShapeDtypeStruct((blocks, rows, columns), values.dtype),
        compiler_params=PARAMS,
    )(values)


def feed_out_kernel(first, second, gate, up, down):
    feed = gate.shape[1]
    gate[...] = first[:, :feed]
    up[...] = second[:, :feed]
    rows, width = down.shape
    parts = [unfold(part[:, feed:], rows, width // 2) for part in (first, second)]
    down[...] = jnp.concatenate(parts, axis=1)


def feed_out(first, second, feed, down_rows, width):
    rows = first.shape[0]
    return pl.pallas_call(
        feed_out_kernel,
        out_shape=[
            jax.ShapeDtypeStruct((rows, feed), F32),
            jax.ShapeDtypeStruct((rows, feed), F32),
            jax.ShapeDtypeStruct((down_rows, width), F32),
        ],
        compiler_params=PARAMS,
    )(first, second)


def weights_out_kernel(first, second, *outs):
    half = first.shape[1] // len(outs)
    for i, out in enumerate(outs):
        pieces = [part[:, i * half : (i + 1) * half] for part in (first, second)]
        out[...] = jnp.concatenate(pieces, axis=1)


def weights_out(first, second):
    rows, columns = first.shape
    return pl.pallas_call(
        weights_out_kernel,
        out_shape=[jax.ShapeDtypeStruct((rows, columns // 2), F32)] * 4,
        compiler_params=PARAMS,
    )(first, second)


def line_buckets(buckets, span_rows, table_rows):
    place = jnp.arange(2 * LANES, dtype=jnp.int32)
    place = jnp.where(place < LANES, place, place - 2 * LANES)
    distance = jnp.arange(3, dtype=jnp.int32)[:, None] * span_rows - place[None, :]
    known = buckets.shape[0]
    hits = distance[:, :, None] == jnp.arange(known, dtype=jnp.int32)
    bucket = jnp.sum(jnp.where(hits, buckets, 0), axis=-1)
    bucket = jnp.where(distance >= known, table_rows - 1, bucket)
    onehot = bucket[:, :, None] == jnp.arange(table_rows, dtype=jnp.int32)
    return (onehot & (distance >= 0)[:, :, None]).astype(F32), distance >= 0


def bias_lines(table, onehot, valid, pair):
    heads = table.shape[1]
    lines = jnp.einsum("kmb,bh->hkm", onehot, table, precision=PRECISE)
    lines = jnp.where(valid[None], lines, MASKED)
    last = jnp.broadcast_to(table[-1][:, None, None], (heads, 1, lines.shape[2]))
    lines = jnp.concatenate((lines, last), axis=1)
    return lines.reshape(heads // pair, pair * 4, lines.shape[2])


def table_gradient(lines, onehot, heads):
    lines = lines.reshape(heads, 4, lines.shape[2])
    grads = jnp.einsum("hkm,kmb->bh", lines[:, :3], onehot, precision=PRECISE)
    return grads.at[-1].add(jnp.sum(lines[:, 3], axis=-1))


def block_kinds(span_order, first_span, query_spans):
    own = lax.dynamic_slice_in_dim(span_order, first_span, query_spans, 0)
    apart = own[:, None] - span_order[None, :]
    kinds = jnp.where(apart < 0, 0, jnp.where(apart > 2, 4, apart + 1))
    return kinds.reshape(-1).astype(jnp.int32)


def per_device(
    inputs,
    encoder_states,
    cotangent,
    span_order,
    buckets,
    gain_self,
    self_query,
    self_key,
    self_value,
    self_out,
    gain_cross,
    cross_query,
    cross_key,
    cross_value,
    cross_out,
    gain_feed,
    feed_gate,
    feed_up,
    feed_down,
    bias_table,
):
    shards, slots = lax.axis_size("shard"), lax.axis_size("ctx")
    shard_rows, width = self_query.shape
    down_rows = feed_down.shape[0]
    feed = feed_gate.shape[1]
    quads = slots == 4 and shards == 8 and shard_rows % 8 == 0 and down_rows % 8 == 0
    token_rows = inputs.shape[1]
    heads = bias_table.shape[1]
    head_size = width // heads
    pair = LANES // head_size
    table_rows = bias_table.shape[0]
    span_rows = token_rows // 2
    slot = lax.axis_index("ctx")
    enc_rows = encoder_states.shape[1]

    gains = jnp.stack((gain_self, gain_cross, gain_feed), axis=1)
    gains = jnp.pad(gains, ((0, 0), (0, LANES - gains.shape[1])))
    mine = [
        self_query,
        self_key,
        self_value,
        self_out,
        cross_query,
        cross_key,
        cross_value,
        cross_out,
        gains,
        feed_gate,
        feed_up,
    ]
    if quads:
        mine = pack_weights(mine, feed_down, shard_rows)
    else:
        mine = jnp.concatenate(mine, axis=1)
    packed = lax.all_gather(mine, BOTH, axis=0, tiled=True)

    def columns(first, last):
        return lax.slice_in_dim(packed, first, last, axis=1)

    w_query, w_key_value = columns(0, width), columns(width, 3 * width)
    w_out, w_cross_query = columns(3 * width, 4 * width), columns(4 * width, 5 * width)
    w_cross_key_value, w_cross_out = columns(5 * width, 7 * width), columns(7 * width, 8 * width)
    base = 8 * width + LANES
    gain_rows = columns(8 * width, base).T.astype(F32)
    g_self, g_cross, g_feed = gain_rows[0], gain_rows[1], gain_rows[2]
    w_gate, w_up = columns(base, base + feed), columns(base + feed, base + 2 * feed)
    if quads:
        folded = columns(base + 2 * feed, packed.shape[1])
        folded = folded.reshape(shards * slots, shard_rows, folded.shape[1])
        w_down = move_tiles(folded, down_rows, width, False).reshape(feed, width)
    else:
        w_down = lax.all_gather(feed_down, BOTH, axis=0, tiled=True)

    sequence = ctx_gather(jnp.concatenate((inputs[0], encoder_states[0]), axis=0), quads)
    sequence = sequence.reshape(slots, token_rows + enc_rows, width)
    tokens_all = sequence[:, :token_rows].reshape(slots * token_rows, width).astype(F32)
    encoded = sequence[:, token_rows:].reshape(slots * enc_rows, width)

    onehot, valid = line_buckets(buckets, span_rows, table_rows)
    lines = bias_lines(bias_table, onehot, valid, pair)
    kinds = block_kinds(span_order, slot * 2, 2)

    tokens = inputs[0].astype(F32)
    unit_all = tokens_all * inverse_norm(tokens_all)
    normed_all = (unit_all * g_self).astype(BF16)
    inverse_self = inverse_norm(tokens)
    unit_self = tokens * inverse_self
    normed_self = (unit_self * g_self).astype(BF16)
    queries = project(normed_self, w_query).astype(BF16)
    keys_values = project(normed_all, w_key_value).astype(BF16)
    probs, attended = self_forward(kinds, queries, keys_values, lines, span_rows, head_size)
    after_self = tokens + project(attended, w_out)
    inverse_cross = inverse_norm(after_self)
    unit_cross = after_self * inverse_cross
    normed_cross = (unit_cross * g_cross).astype(BF16)
    cross_q = project(normed_cross, w_cross_query).astype(BF16)
    cross_kv = project(encoded, w_cross_key_value).astype(BF16)
    cross_probs, cross_att = cross_forward(cross_q, cross_kv, head_size)
    after_cross = after_self + project(cross_att, w_cross_out)
    inverse_feed = inverse_norm(after_cross)
    unit_feed = after_cross * inverse_feed
    normed_feed = (unit_feed * g_feed).astype(BF16)
    gate_pre = project(normed_feed, w_gate)
    up_pre = project(normed_feed, w_up)
    gated, gated_pull = jax.vjp(
        lambda first, second: jax.nn.gelu(first, approximate=True) * second, gate_pre, up_pre
    )
    hidden = gated.astype(BF16)
    outputs = (after_cross + project(hidden, w_down)).astype(BF16)

    grad_out = cotangent[0]
    outer = grad_out.astype(F32)
    if quads:
        core = slot % 2
        out_keep, out_send = core_halves(grad_out)
        lefts = swap(
            jnp.concatenate(
                (attended, normed_cross, cross_att, normed_feed, hidden, out_send), axis=1
            ),
            1,
        )

    def pair_sum(left, left_in, right, right_in):
        return outer_sum(
            jnp.concatenate((left, left_in), axis=0), jnp.concatenate((right, right_in), axis=0)
        ).astype(BF16)

    grad_gate, grad_up = gated_pull(project_back(grad_out, w_down))
    grad_gate, grad_up = grad_gate.astype(BF16), grad_up.astype(BF16)
    if quads:
        keep = jnp.where(core == 0, grad_gate, grad_up)
        arrived = swap(jnp.where(core == 0, grad_up, grad_gate), 1)
    grad_normed = project_back(grad_gate, w_gate) + project_back(grad_up, w_up)
    gain_feed_grad = jnp.sum(grad_normed * unit_feed, axis=0)
    grad_cross_out = outer + norm_back(after_cross, inverse_feed, g_feed, grad_normed)
    grad_low_cross = grad_cross_out.astype(BF16)
    grad_att = project_back(grad_low_cross, w_cross_out).astype(BF16)
    if quads:
        base = 4 * width
        down_part = pair_sum(hidden, lefts[:, base : base + feed], out_keep, lefts[:, base + feed :])
        down_part = move_tiles(
            down_part.reshape(shards * slots, down_rows, width // 2),
            shard_rows,
            down_rows * width // 2 // shard_rows,
            True,
        ).reshape(width, -1)
        cut = (feed + down_part.shape[1]) // 2
        feed_lefts = (normed_feed, lefts[:, 3 * width : 4 * width])
        feed_left = pair_sum(*feed_lefts, keep[:, :cut], arrived[:, :cut])
        feed_right = pair_sum(*feed_lefts, keep[:, cut:], arrived[:, cut:])
        feed_right = jnp.concatenate((feed_right, down_part), axis=1)
        grad_att, *feed_sends = tied(grad_att, *plane_sends(feed_left, feed_right))
        feed_in = plane_first(*feed_sends[:2])
    else:
        own_down = scatter_sum(outer_sum(hidden, grad_out).astype(BF16))
        own_gate = scatter_sum(outer_sum(normed_feed, grad_gate).astype(BF16))
        own_up = scatter_sum(outer_sum(normed_feed, grad_up).astype(BF16))

    groups = width // LANES
    half_groups = groups // 2 if quads else groups

    def scalars_at(kind_scalars, group):
        return jnp.concatenate((kind_scalars, jnp.reshape(group, (1,)).astype(jnp.int32)))

    def in_order(kept, sent, axis):
        if not quads:
            return kept
        first, second = jnp.where(core == 0, kept, sent), jnp.where(core == 0, sent, kept)
        return jnp.concatenate((first, second), axis=axis)

    def attention_sums(kept, arrived, result, lefts_q, lefts_o, keys_from):
        half = width // 2
        left = jnp.concatenate(
            (
                pair_sum(*lefts_q, kept[0], arrived[0][:, :half]),
                pair_sum(*lefts_o, result, arrived[0][:, half:]),
            ),
            axis=1,
        )
        keys_values_sum = add_low(kept[1], arrived[1])
        right = jnp.concatenate((keys_values_sum[0], keys_values_sum[1]), axis=1)
        return left, outer_sum(keys_from, right).astype(BF16)

    none = jnp.zeros((0,), jnp.int32)
    if quads:
        result_keep, result_send = core_halves(grad_low_cross)
        sent = cross_backward(
            scalars_at(none, (1 - core) * half_groups),
            half_groups,
            cross_q,
            grad_att,
            cross_kv,
            cross_probs,
            head_size,
        )
        arrived = (
            swap(jnp.concatenate((sent[0], result_send), axis=1), 1),
            swap(sent[1], 1),
        )
        grad_att, *sent = tied(grad_att, *sent)
    kept = cross_backward(
        scalars_at(none, core * half_groups if quads else jnp.int32(0)),
        half_groups,
        cross_q,
        grad_att,
        cross_kv,
        cross_probs,
        head_size,
    )
    if not quads:
        sent = kept
    grad_cq = in_order(kept[0], sent[0], 1)
    grad_normed = project_back(grad_cq, w_cross_query)
    gain_cross_grad = jnp.sum(grad_normed * unit_cross, axis=0)
    grad_self_out = grad_cross_out + norm_back(after_self, inverse_cross, g_cross, grad_normed)
    grad_low_self = grad_self_out.astype(BF16)
    grad_att = project_back(grad_low_self, w_out).astype(BF16)
    cross_kept, cross_sent = kept[1], sent[1]

    if quads:
        cross_parts = attention_sums(
            kept,
            arrived,
            result_keep,
            (normed_cross, lefts[:, width : 2 * width]),
            (cross_att, lefts[:, 2 * width : 3 * width]),
            encoded,
        )
        grad_att, *cross_sends = tied(grad_att, *plane_sends(*cross_parts))
        cross_in = plane_first(*cross_sends[:2])
        result_keep, result_send = core_halves(grad_low_self)
        sent = self_backward(
            scalars_at(kinds, (1 - core) * half_groups),
            half_groups,
            queries,
            grad_att,
            keys_values,
            probs,
            span_rows,
            head_size,
        )
        arrived = (
            swap(jnp.concatenate((sent[0], result_send), axis=1), 1),
            swap(sent[1], 1),
        )
        joint = tied(grad_att, *feed_in, *cross_in, *sent)
        grad_att, feed_in, cross_in, sent = joint[0], joint[1:3], joint[3:5], joint[5:]
        feed_sends = plane_second_sends(feed_sends[2], feed_in[0], feed_sends[3], feed_in[1])
        cross_sends = plane_second_sends(cross_sends[2], cross_in[0], cross_sends[3], cross_in[1])
        grad_att, *joint = tied(grad_att, *feed_sends, *cross_sends)
        feed_sends, cross_sends = joint[:4], joint[4:]
        feed_in = plane_second(*feed_sends[:2])
        cross_in = plane_second(*cross_sends[:2])
    kept = self_backward(
        scalars_at(kinds, core * half_groups if quads else jnp.int32(0)),
        half_groups,
        queries,
        grad_att,
        keys_values,
        probs,
        span_rows,
        head_size,
    )
    if not quads:
        sent = kept
    if quads:
        joint = tied(*feed_in, *cross_in, *kept)
        feed_in, cross_in, kept = joint[:2], joint[2:4], joint[4:]
        first_plane = jnp.concatenate(
            (
                plane_sum(feed_sends[2], feed_in[0], feed_sends[3], feed_in[1]),
                plane_sum(cross_sends[2], cross_in[0], cross_sends[3], cross_in[1]),
            ),
            axis=2,
        )
        partner = lax.dynamic_slice_in_dim(normed_all, (slot ^ 1) * token_rows, token_rows, 0)
        self_parts = attention_sums(
            kept,
            arrived,
            result_keep,
            (normed_self, partner),
            (attended, lefts[:, :width]),
            normed_all,
        )
        joint = tied(*plane_sends(*self_parts), *z_sends(first_plane), cross_kept, *kept)
        self_sends, first_sends = joint[:4], joint[4 : 4 + first_plane.shape[0]]
        cross_kept, *kept = joint[4 + first_plane.shape[0] :]
        self_in = plane_first(*self_sends[:2])
        first_in = z_swaps(first_sends)
    grad_q = in_order(kept[0], sent[0], 1)
    part_kv = in_order(kept[1], sent[1], 2)
    part_kv = jnp.concatenate((part_kv[0], part_kv[1]), axis=1)
    part_ckv = in_order(cross_kept, cross_sent, 2)
    part_ckv = jnp.concatenate((part_ckv[0], part_ckv[1]), axis=1)
    grad_lines = in_order(kept[2], sent[2], 0)
    grad_kv_normed = project_back(part_kv, w_key_value)
    grad_q_normed = project_back(grad_q, w_query)
    gain_self_grad = jnp.sum(grad_kv_normed * unit_all, axis=0) + jnp.sum(
        grad_q_normed * unit_self, axis=0
    )
    to_encoder = project_back(part_ckv, w_cross_key_value).astype(BF16)
    to_inputs = grad_kv_normed.astype(BF16)
    if quads:
        joint = tied(*self_in, gain_self_grad, grad_lines)
        self_in, (gain_self_grad, grad_lines) = joint[:2], joint[2:]
        self_sends = plane_second_sends(self_sends[2], self_in[0], self_sends[3], self_in[1])
        self_in = plane_second(*self_sends[:2])
    else:
        cross_query_grad = scatter_sum(outer_sum(normed_cross, grad_cq).astype(BF16))
        cross_out_grad = scatter_sum(outer_sum(cross_att, grad_low_cross).astype(BF16))
        cross_key_grad = scatter_sum(outer_sum(encoded, cross_kept[0]).astype(BF16))
        cross_value_grad = scatter_sum(outer_sum(encoded, cross_kept[1]).astype(BF16))
        query_grad = scatter_sum(outer_sum(normed_self, grad_q).astype(BF16))
        self_out_grad = scatter_sum(outer_sum(attended, grad_low_self).astype(BF16))
        key_grad = scatter_sum(outer_sum(normed_all, kept[1][0]).astype(BF16))
        value_grad = scatter_sum(outer_sum(normed_all, kept[1][1]).astype(BF16))
    table_part = table_gradient(grad_lines, onehot, heads)
    small = jnp.concatenate(
        (gain_self_grad, gain_cross_grad, gain_feed_grad, table_part.reshape(-1))
    )
    tile = 8 * LANES
    extent = small.shape[0]
    small = jnp.pad(small, (0, -extent % tile)).reshape(-1, LANES)
    if quads:
        joint = tied(*self_in, *first_in, small_plane_sum(small), to_encoder, to_inputs)
        self_in, first_in = joint[:2], joint[2 : 1 + len(first_sends)]
        small, to_encoder, to_inputs = joint[1 + len(first_sends) :]
        self_sends = z_sends(
            plane_sum(self_sends[2], self_in[0], self_sends[3], self_in[1])
        )
        self_in = z_swaps(self_sends)
        first, second = between_cores(z_total(first_sends[0], first_in))
        split = first.shape[1] - 2 * width
        own_gate, own_up, own_down = feed_out(
            first[:, :split], second[:, :split], feed, down_rows, width
        )
        cross_query_grad, cross_out_grad, cross_key_grad, cross_value_grad = weights_out(
            first[:, split:], second[:, split:]
        )
        small = small_z_sum(small)
    else:
        small = lax.psum(small, BOTH)
    encoder_grad = ctx_scatter_sum(to_encoder, quads)
    to_inputs = ctx_scatter_sum(to_inputs, quads)
    if quads:
        small, encoder_grad, to_inputs, *self_in = tied(small, encoder_grad, to_inputs, *self_in)
        query_grad, self_out_grad, key_grad, value_grad = weights_out(
            *between_cores(z_total(self_sends[0], self_in))
        )
    grad_normed = grad_q_normed + to_inputs
    input_grad = grad_self_out + norm_back(tokens, inverse_self, g_self, grad_normed)
    small = small.reshape(-1)
    position = lax.axis_index(BOTH) * shard_rows
    own_gains = [
        lax.dynamic_slice_in_dim(small, i * width + position, shard_rows, 0) for i in range(3)
    ]
    table_total = small[3 * width : extent].reshape(table_rows, heads)
    return (
        outputs[None],
        input_grad.astype(BF16)[None],
        encoder_grad.astype(BF16)[None],
        own_gains[0],
        query_grad,
        key_grad,
        value_grad,
        self_out_grad,
        own_gains[1],
        cross_query_grad,
        cross_key_grad,
        cross_value_grad,
        cross_out_grad,
        own_gains[2],
        own_gate,
        own_up,
        own_down,
        table_total,
    )


def solution(mesh):
    in_specs = (
        P("shard", "ctx", None),
        P("shard", "ctx", None),
        P("shard", "ctx", None),
        P(),
        P(),
        P(("shard", "ctx")),
        P(("shard", "ctx"), None),
        P(("shard", "ctx"), None),
        P(("shard", "ctx"), None),
        P(("shard", "ctx"), None),
        P(("shard", "ctx")),
        P(("shard", "ctx"), None),
        P(("shard", "ctx"), None),
        P(("shard", "ctx"), None),
        P(("shard", "ctx"), None),
        P(("shard", "ctx")),
        P(("shard", "ctx"), None),
        P(("shard", "ctx"), None),
        P(("shard", "ctx"), None),
        P(),
    )
    out_specs = (
        P("shard", "ctx", None),
        P("shard", "ctx", None),
        P("shard", "ctx", None),
        P(("shard", "ctx")),
        P(("shard", "ctx"), None),
        P(("shard", "ctx"), None),
        P(("shard", "ctx"), None),
        P(("shard", "ctx"), None),
        P(("shard", "ctx")),
        P(("shard", "ctx"), None),
        P(("shard", "ctx"), None),
        P(("shard", "ctx"), None),
        P(("shard", "ctx"), None),
        P(("shard", "ctx")),
        P(("shard", "ctx"), None),
        P(("shard", "ctx"), None),
        P(("shard", "ctx"), None),
        P(),
    )
    return jax.shard_map(
        per_device, mesh=mesh, in_specs=in_specs, out_specs=out_specs, check_vma=False
    )
```

```python
import functools

import jax
import jax.numpy as jnp
from jax import lax
from jax.experimental import pallas as pl
from jax.experimental.pallas import tpu as pltpu
from jax.sharding import PartitionSpec as P

EPSILON = 1e-06
MASKED = -1e30
PRECISE = lax.Precision.HIGHEST
LANES = 128
BOTH = ("shard", "ctx")
F32 = jnp.float32
BF16 = jnp.bfloat16


def inverse_norm(values):
    return lax.rsqrt(jnp.mean(values * values, axis=-1, keepdims=True) + EPSILON)


def norm_back(values, inverse, gain, grads):
    weighted = gain * grads
    middle = jnp.mean(weighted * values, axis=-1, keepdims=True)
    return inverse * weighted - values * (inverse * inverse * inverse) * middle


def project(left, right):
    return jnp.dot(left, right, preferred_element_type=F32)


def project_back(grads, weight):
    return lax.dot_general(grads, weight, (((1,), (1,)), ((), ())), preferred_element_type=F32)


def outer_sum(left, grads):
    return lax.dot_general(left, grads, (((0,), (0,)), ((), ())), preferred_element_type=F32)


def swap(values, mask):
    count = lax.axis_size("shard") * lax.axis_size("ctx")
    return lax.ppermute(values, BOTH, [(i, i ^ mask) for i in range(count)])


def pick(values, index, axis):
    return lax.dynamic_index_in_dim(values, index, axis, keepdims=False)


def paired(first, second, flag):
    joined = jnp.concatenate((first, second), axis=0)
    return jnp.where(flag == 0, joined, jnp.concatenate((second, first), axis=0))


def ctx_gather(values, quads):
    if not quads:
        return lax.all_gather(values, "ctx", axis=0, tiled=True)
    slot = lax.axis_index("ctx")
    far = swap(values, 2)
    near = paired(values, swap(values, 1), slot % 2)
    far = paired(far, swap(far, 1), slot % 2)
    return paired(near, far, slot // 2)


def ctx_scatter_sum(values, quads):
    if not quads:
        return lax.psum_scatter(values, "ctx", scatter_dimension=0, tiled=True).astype(F32)
    slot = lax.axis_index("ctx")
    core, row = slot % 2, slot // 2
    parts = values.reshape(2, 2, values.shape[0] // 4, values.shape[1])
    summed = pick(parts, core, 1).astype(F32) + swap(pick(parts, 1 - core, 1), 1).astype(F32)
    summed = summed.astype(BF16)
    return pick(summed, row, 0).astype(F32) + swap(pick(summed, 1 - row, 0), 2).astype(F32)


def place():
    shard, ctx = lax.axis_index("shard"), lax.axis_index("ctx")
    return ctx % 2, ctx // 2, shard % 2, shard // 2


def add_low(first, second):
    return (first.astype(F32) + second.astype(F32)).astype(BF16)


def by_chip(values):
    layers = lax.axis_size("shard") // 2
    return values.reshape(layers, 2, 2, values.shape[0] // (layers * 4), values.shape[1])


def plane_sends(left, right):
    _, row, column, _ = place()
    left, right = by_chip(left), by_chip(right)
    sends = pick(left, 1 - column, 1), pick(right, 1 - row, 2)
    return sends + (pick(left, column, 1), pick(right, row, 2))


def plane_first(left_out, right_out):
    return swap(left_out, 4), swap(right_out, 2)


def plane_second_sends(left, left_in, right, right_in):
    _, row, column, _ = place()
    left, right = add_low(left, left_in), add_low(right, right_in)
    sends = pick(left, 1 - row, 1), pick(right, 1 - column, 1)
    return sends + (pick(left, row, 1), pick(right, column, 1))


def plane_second(left_out, right_out):
    return swap(left_out, 2), swap(right_out, 4)


def plane_sum(left, left_in, right, right_in):
    return jnp.concatenate((add_low(left, left_in), add_low(right, right_in)), axis=-1)


def z_sends(plane):
    layer = lax.axis_index("shard") // 2
    return [pick(plane, layer ^ step, 0) for step in range(plane.shape[0])]


def z_swaps(parts):
    return [swap(part, 8 * step) for step, part in enumerate(parts) if step]


def z_total(own, arrived):
    total = own.astype(F32)
    for part in arrived:
        total = total + part.astype(F32)
    return total


def between_cores(total):
    core = lax.axis_index("ctx") % 2
    total = total.reshape(2, total.shape[0] // 2, total.shape[1])
    own = pick(total, core, 0)
    other = swap(pick(total, 1 - core, 0).astype(BF16), 1).astype(F32)
    return jnp.where(core == 0, own, other), jnp.where(core == 0, other, own)


def core_halves(values):
    core = lax.axis_index("ctx") % 2
    half = values.shape[1] // 2
    low, high = values[:, :half], values[:, half:]
    return jnp.where(core == 0, low, high), jnp.where(core == 0, high, low)


def chip_rows(first, second):
    core, _, _, _ = place()
    mine, theirs = jnp.where(core == 0, first, second), jnp.where(core == 0, second, first)
    return paired(mine, swap(theirs, 1), core)


def z_gather(chip):
    return [swap(chip, 8 * step) for step in range(1, lax.axis_size("shard") // 2)]


def z_ordered(chip, arrived):
    layer = lax.axis_index("shard") // 2
    stacked = jnp.stack([chip, *arrived])
    stacked = jnp.stack([pick(stacked, layer ^ step, 0) for step in range(stacked.shape[0])])
    half = chip.shape[1] // 2 // LANES * LANES
    return stacked[..., :half], stacked[..., half:]


def joined(mine, theirs, flag, axis):
    low, high = jnp.where(flag == 0, mine, theirs), jnp.where(flag == 0, theirs, mine)
    return jnp.stack((low, high), axis=axis)


def plane_gathered_first(left, right, left_in, right_in):
    _, row, column, _ = place()
    return joined(left, left_in, column, 1), joined(right, right_in, row, 1)


def plane_gathered(left, right, left_in, right_in):
    _, row, column, _ = place()
    left, right = joined(left, left_in, row, 2), joined(right, right_in, column, 1)
    own = jnp.concatenate((left, right), axis=-1)
    return own.reshape(-1, own.shape[-1])


def tied(value, *others):
    return lax.optimization_barrier((value,) + others)


def scatter_sum(values):
    return lax.psum_scatter(values, BOTH, scatter_dimension=0, tiled=True).astype(F32)


def small_plane_sum(values):
    for mask in (1, 2, 4):
        values = values + swap(values, mask)
    return values


def small_z_sum(values):
    arrived = [swap(values, 8 * step) for step in range(1, lax.axis_size("shard") // 2)]
    layer = lax.axis_index("shard") // 2
    stacked = jnp.stack([values] + arrived)
    return sum(pick(stacked, layer ^ step, 0) for step in range(stacked.shape[0]))


def fold(values, rows, columns):
    lead = values.shape[:-2]
    tall, wide = values.shape[-2] // 8, rows // 8
    step = values.shape[-1] // wide
    cut = values.reshape(lead + (tall, 8, values.shape[-1]))
    bands = []
    for band in range(wide):
        bands.append(
            jnp.concatenate(
                [cut[..., t, :, band * step : (band + 1) * step] for t in range(tall)], axis=-1
            )
        )
    return jnp.concatenate(bands, axis=-2)


def unfold(values, rows, columns):
    tall, wide = rows // 8, values.shape[-2] // 8
    step = columns // wide
    out = []
    for t in range(tall):
        out.append(
            jnp.concatenate(
                [
                    values[..., w * 8 : (w + 1) * 8, t * step : (t + 1) * step]
                    for w in range(wide)
                ],
                axis=-1,
            )
        )
    return jnp.concatenate(out, axis=-2)


def head_mask(shape, head_size, head):
    lane = lax.broadcasted_iota(jnp.int32, shape, 1)
    return lane // head_size == head


def pad_keys(source, target, span_rows):
    spans = source.shape[0] // span_rows
    for b in range(spans):
        target[b * LANES : b * LANES + span_rows, :] = source[
            b * span_rows : (b + 1) * span_rows, :
        ]


def skew(values, right):
    width = values.shape[1]
    row = lax.broadcasted_iota(jnp.int32, values.shape, 0)
    for bit in range((values.shape[0] - 1).bit_length()):
        shift = 1 << bit
        moved = pltpu.roll(values, shift if right else width - shift, 1)
        values = jnp.where((row >> bit) & 1 == 1, moved, values)
    return values


def dot_rows(left, right):
    return lax.dot_general(left, right, (((1,), (1,)), ((), ())), preferred_element_type=F32)


def dot_columns(left, right):
    return lax.dot_general(left, right, (((0,), (0,)), ((), ())), preferred_element_type=F32)


def probabilities(scores):
    top = jnp.max(scores, axis=1, keepdims=True)
    raised = jnp.exp(scores - top)
    return raised * (1.0 / jnp.sum(raised, axis=1, keepdims=True))


def self_forward_kernel(
    kind_ref, q_ref, k_ref, v_ref, line_ref, p_ref, o_ref, kp, vp, tables, s_ref, *, span_rows, head_size
):
    @pl.when(pl.program_id(0) == 0)
    def _():
        kp[...] = jnp.zeros(kp.shape, kp.dtype)
        vp[...] = jnp.zeros(vp.shape, vp.dtype)

    pad_keys(k_ref, kp, span_rows)
    pad_keys(v_ref, vp, span_rows)
    pair = LANES // head_size
    spans = k_ref.shape[0] // span_rows
    query_spans = q_ref.shape[0] // span_rows
    inside = lax.broadcasted_iota(jnp.int32, (span_rows, LANES), 1) < span_rows
    out = jnp.zeros(o_ref.shape, F32)
    for h in range(pair):
        tables[0] = jnp.full((span_rows, LANES), MASKED, F32)
        for k in range(4):
            line = jnp.broadcast_to(
                line_ref[0, h * 4 + k : h * 4 + k + 1, :], (span_rows, 2 * LANES)
            )
            if k < 3:
                line = skew(line, True)
            tables[k + 1] = jnp.where(inside, line[:, :LANES], MASKED)
        q = jnp.where(head_mask(q_ref.shape, head_size, h), q_ref[...], jnp.zeros((), BF16))
        s_ref[...] = dot_rows(q, kp[...]) * (head_size**-0.5)
        for a in range(query_spans):
            for b in range(spans):
                rows, columns = pl.ds(a * span_rows, span_rows), pl.ds(b * LANES, LANES)
                s_ref[rows, columns] = s_ref[rows, columns] + tables[kind_ref[a * spans + b]]
        probs = probabilities(s_ref[...]).astype(BF16)
        p_ref[h] = probs
        v = jnp.where(head_mask(vp.shape, head_size, h), vp[...], jnp.zeros((), BF16))
        out = out + jnp.dot(probs, v, preferred_element_type=F32)
    o_ref[...] = out.astype(BF16)


def cross_forward_kernel(q_ref, k_ref, v_ref, p_ref, o_ref, *, head_size):
    out = jnp.zeros(o_ref.shape, F32)
    for h in range(LANES // head_size):
        q = jnp.where(head_mask(q_ref.shape, head_size, h), q_ref[...], jnp.zeros((), BF16))
        probs = probabilities(dot_rows(q, k_ref[...]) * (head_size**-0.5)).astype(BF16)
        p_ref[h] = probs
        v = jnp.where(head_mask(v_ref.shape, head_size, h), v_ref[...], jnp.zeros((), BF16))
        out = out + jnp.dot(probs, v, preferred_element_type=F32)
    o_ref[...] = out.astype(BF16)


def pair_backward(h, q_ref, do_ref, keys, values, p_ref, head_size):
    grads = jnp.where(head_mask(do_ref.shape, head_size, h), do_ref[...], jnp.zeros((), BF16))
    q = jnp.where(head_mask(q_ref.shape, head_size, h), q_ref[...], jnp.zeros((), BF16))
    probs_low = p_ref[h]
    probs = probs_low.astype(F32)
    grad_probs = dot_rows(grads, values)
    delta = jnp.sum(probs * grad_probs, axis=1, keepdims=True)
    grad_scores = (probs * (grad_probs - delta)).astype(BF16)
    k = jnp.where(head_mask(keys.shape, head_size, h), keys, jnp.zeros((), BF16))
    grad_q = jnp.dot(grad_scores, k, preferred_element_type=F32)
    return grad_scores, grad_q, dot_columns(grad_scores, q), dot_columns(probs_low, grads)


def self_backward_kernel(
    kind_ref,
    q_ref,
    do_ref,
    k_ref,
    v_ref,
    p_ref,
    dq_ref,
    dkv_ref,
    line_ref,
    kp,
    vp,
    tables,
    s_ref,
    *,
    span_rows,
    head_size,
):
    @pl.when(pl.program_id(0) == 0)
    def _():
        kp[...] = jnp.zeros(kp.shape, kp.dtype)
        vp[...] = jnp.zeros(vp.shape, vp.dtype)

    pad_keys(k_ref, kp, span_rows)
    pad_keys(v_ref, vp, span_rows)
    pair = LANES // head_size
    spans = k_ref.shape[0] // span_rows
    query_spans = q_ref.shape[0] // span_rows
    scale = head_size**-0.5
    grad_q = jnp.zeros(dq_ref.shape, F32)
    grad_k = jnp.zeros(kp.shape, F32)
    grad_v = jnp.zeros(vp.shape, F32)
    blank = jnp.zeros((span_rows, LANES), F32)
    for h in range(pair):
        scores, part_q, part_k, part_v = pair_backward(
            h, q_ref, do_ref, kp[...], vp[...], p_ref, head_size
        )
        grad_q, grad_k, grad_v = grad_q + part_q, grad_k + part_k, grad_v + part_v
        s_ref[...] = scores.astype(F32)
        tables[...] = jnp.zeros(tables.shape, F32)
        for a in range(query_spans):
            for b in range(spans):
                kind = kind_ref[a * spans + b]
                rows, columns = pl.ds(a * span_rows, span_rows), pl.ds(b * LANES, LANES)
                tables[kind] = tables[kind] + s_ref[rows, columns]
        for k in range(4):
            block = jnp.concatenate((tables[k + 1], blank), axis=1)
            if k < 3:
                block = skew(block, False)
            line_ref[0, h * 4 + k : h * 4 + k + 1, :] = jnp.sum(block, axis=0, keepdims=True)
    dq_ref[...] = (grad_q * scale).astype(BF16)
    grad_k = (grad_k * scale).astype(BF16)
    grad_v = grad_v.astype(BF16)
    for b in range(spans):
        target, source = pl.ds(b * span_rows, span_rows), slice(b * LANES, b * LANES + span_rows)
        dkv_ref[0, target, :] = grad_k[source]
        dkv_ref[1, target, :] = grad_v[source]


def cross_backward_kernel(
    _, q_ref, do_ref, k_ref, v_ref, p_ref, dq_ref, dkv_ref, *, head_size
):
    scale = head_size**-0.5
    grad_q = jnp.zeros(dq_ref.shape, F32)
    grad_k = jnp.zeros(k_ref.shape, F32)
    grad_v = jnp.zeros(v_ref.shape, F32)
    for h in range(LANES // head_size):
        _, part_q, part_k, part_v = pair_backward(
            h, q_ref, do_ref, k_ref[...], v_ref[...], p_ref, head_size
        )
        grad_q, grad_k, grad_v = grad_q + part_q, grad_k + part_k, grad_v + part_v
    dq_ref[...] = (grad_q * scale).astype(BF16)
    dkv_ref[0] = (grad_k * scale).astype(BF16)
    dkv_ref[1] = grad_v.astype(BF16)


PARAMS = pltpu.CompilerParams(vmem_limit_bytes=48 * 1024 * 1024)


def columns_of(rows, offset=0):
    return pl.BlockSpec((rows, LANES), lambda g, *_: (0, g + offset))


def probs_spec(pair, rows, keys):
    return pl.BlockSpec((pair, rows, keys), lambda g, *_: (g, 0, 0))


def lines_spec():
    return pl.BlockSpec((1, 8, 2 * LANES), lambda g, *_: (g, 0, 0))


def self_forward(kinds, queries, keys_values, lines, span_rows, head_size):
    rows, width = queries.shape
    key_rows = keys_values.shape[0]
    groups, pair = width // LANES, LANES // head_size
    padded = key_rows // span_rows * LANES
    return pl.pallas_call(
        functools.partial(self_forward_kernel, span_rows=span_rows, head_size=head_size),
        grid_spec=pltpu.PrefetchScalarGridSpec(
            num_scalar_prefetch=1,
            grid=(groups,),
            in_specs=[
                columns_of(rows),
                columns_of(key_rows),
                columns_of(key_rows, groups),
                lines_spec(),
            ],
            out_specs=[probs_spec(pair, rows, padded), columns_of(rows)],
            scratch_shapes=[
                pltpu.VMEM((padded, LANES), BF16),
                pltpu.VMEM((padded, LANES), BF16),
                pltpu.VMEM((5, span_rows, LANES), F32),
                pltpu.VMEM((rows, padded), F32),
            ],
        ),
        out_shape=[
            jax.ShapeDtypeStruct((groups * pair, rows, padded), BF16),
            jax.ShapeDtypeStruct((rows, width), BF16),
        ],
        compiler_params=PARAMS,
    )(kinds, queries, keys_values, keys_values, lines)


def backward_specs(rows, key_rows, padded, groups, pair):
    def at(offset=0):
        return lambda g, scalars: (0, g + scalars[scalars.shape[0] - 1] + offset)

    ins = [
        pl.BlockSpec((rows, LANES), at()),
        pl.BlockSpec((rows, LANES), at()),
        pl.BlockSpec((key_rows, LANES), at()),
        pl.BlockSpec((key_rows, LANES), at(groups)),
        pl.BlockSpec(
            (pair, rows, padded), lambda g, scalars: (g + scalars[scalars.shape[0] - 1], 0, 0)
        ),
    ]
    outs = [
        pl.BlockSpec((rows, LANES), lambda g, _: (0, g)),
        pl.BlockSpec((2, key_rows, LANES), lambda g, _: (0, 0, g)),
    ]
    return ins, outs


def self_backward(scalars, count, queries, grads, keys_values, probs, span_rows, head_size):
    rows, width = queries.shape
    key_rows = keys_values.shape[0]
    groups, pair = width // LANES, LANES // head_size
    padded = probs.shape[2]
    in_specs, out_specs = backward_specs(rows, key_rows, padded, groups, pair)
    return pl.pallas_call(
        functools.partial(self_backward_kernel, span_rows=span_rows, head_size=head_size),
        grid_spec=pltpu.PrefetchScalarGridSpec(
            num_scalar_prefetch=1,
            grid=(count,),
            in_specs=in_specs,
            out_specs=out_specs + [lines_spec()],
            scratch_shapes=[
                pltpu.VMEM((padded, LANES), BF16),
                pltpu.VMEM((padded, LANES), BF16),
                pltpu.VMEM((5, span_rows, LANES), F32),
                pltpu.VMEM((rows, padded), F32),
            ],
        ),
        out_shape=[
            jax.ShapeDtypeStruct((rows, count * LANES), BF16),
            jax.ShapeDtypeStruct((2, key_rows, count * LANES), BF16),
            jax.ShapeDtypeStruct((count, 8, 2 * LANES), F32),
        ],
        compiler_params=PARAMS,
    )(scalars, queries, grads, keys_values, keys_values, probs)


def cross_backward(scalars, count, queries, grads, keys_values, probs, head_size):
    rows, width = queries.shape
    key_rows = keys_values.shape[0]
    groups, pair = width // LANES, LANES // head_size
    in_specs, out_specs = backward_specs(rows, key_rows, key_rows, groups, pair)
    return pl.pallas_call(
        functools.partial(cross_backward_kernel, head_size=head_size),
        grid_spec=pltpu.PrefetchScalarGridSpec(
            num_scalar_prefetch=1, grid=(count,), in_specs=in_specs, out_specs=out_specs
        ),
        out_shape=[
            jax.ShapeDtypeStruct((rows, count * LANES), BF16),
            jax.ShapeDtypeStruct((2, key_rows, count * LANES), BF16),
        ],
        compiler_params=PARAMS,
    )(scalars, queries, grads, keys_values, keys_values, probs)


def cross_forward(queries, keys_values, head_size):
    rows, width = queries.shape
    key_rows = keys_values.shape[0]
    groups, pair = width // LANES, LANES // head_size
    return pl.pallas_call(
        functools.partial(cross_forward_kernel, head_size=head_size),
        grid=(groups,),
        in_specs=[columns_of(rows), columns_of(key_rows), columns_of(key_rows, groups)],
        out_specs=[probs_spec(pair, rows, key_rows), columns_of(rows)],
        out_shape=[
            jax.ShapeDtypeStruct((groups * pair, rows, key_rows), BF16),
            jax.ShapeDtypeStruct((rows, width), BF16),
        ],
        compiler_params=PARAMS,
    )(queries, keys_values, keys_values)


def pack_kernel(*refs, pieces):
    parts, (gains, down), outs, sems = (
        refs[:pieces],
        refs[pieces : pieces + 2],
        refs[pieces + 2 : pieces + 6],
        refs[pieces + 6],
    )
    width, feed = parts[0].shape[1], parts[-1].shape[1]
    half = (pieces - 2) // 2
    copies = []
    for i, part in enumerate(parts):
        if i < pieces - 2:
            out, start = outs[i // half], i % half * width
        else:
            out, start = outs[2 + i - (pieces - 2)], 0
        target = out.at[:, pl.ds(start, part.shape[1])]
        copies.append(pltpu.make_async_copy(part, target, sems.at[i]))
    for copy in copies:
        copy.start()
    for out in outs[:2]:
        out[:, half * width :] = gains[...]
    middle = down.shape[1] // 2
    for i, out in enumerate(outs[2:]):
        piece = down[:, i * middle : (i + 1) * middle].astype(F32)
        out[:, feed:] = fold(piece, out.shape[0], out.shape[1] - feed).astype(out.dtype)
    for copy in copies:
        copy.wait()


def pack_weights(parts, gains, gate, up, down):
    rows = gate.shape[0]
    half = sum(part.shape[1] for part in parts) // 2 + gains.shape[1]
    feed = gate.shape[1] + down.size // 2 // rows
    far, near = pl.BlockSpec(memory_space=pltpu.HBM), pl.BlockSpec(memory_space=pltpu.VMEM)
    return pl.pallas_call(
        functools.partial(pack_kernel, pieces=len(parts) + 2),
        in_specs=[far] * (len(parts) + 2) + [near, near],
        out_specs=[near] * 4,
        out_shape=[
            jax.ShapeDtypeStruct((rows, columns), gate.dtype)
            for columns in (half, half, feed, feed)
        ],
        scratch_shapes=[pltpu.SemaphoreType.DMA((len(parts) + 2,))],
        compiler_params=PARAMS,
    )(*parts, gate, up, gains, down)


def move_kernel(in_ref, out_ref, *, folding):
    move = fold if folding else unfold
    for i in range(in_ref.shape[0]):
        moved = move(in_ref[i].astype(F32), out_ref.shape[1], out_ref.shape[2])
        out_ref[i] = moved.astype(out_ref.dtype)


def move_tiles(values, rows, columns, folding):
    blocks = values.shape[0]
    step = 8 if blocks % 8 == 0 else 1
    return pl.pallas_call(
        functools.partial(move_kernel, folding=folding),
        grid=(blocks // step,),
        in_specs=[pl.BlockSpec((step,) + values.shape[1:], lambda g: (g, 0, 0))],
        out_specs=pl.BlockSpec((step, rows, columns), lambda g: (g, 0, 0)),
        out_shape=jax.ShapeDtypeStruct((blocks, rows, columns), values.dtype),
        compiler_params=PARAMS,
    )(values)


def feed_out_kernel(first, second, gate, up, down):
    feed = gate.shape[1]
    gate[...] = first[:, :feed]
    up[...] = second[:, :feed]
    rows, width = down.shape
    parts = [unfold(part[:, feed:], rows, width // 2) for part in (first, second)]
    down[...] = jnp.concatenate(parts, axis=1)


def feed_out(first, second, feed, down_rows, width):
    rows = first.shape[0]
    return pl.pallas_call(
        feed_out_kernel,
        out_shape=[
            jax.ShapeDtypeStruct((rows, feed), F32),
            jax.ShapeDtypeStruct((rows, feed), F32),
            jax.ShapeDtypeStruct((down_rows, width), F32),
        ],
        compiler_params=PARAMS,
    )(first, second)


def weights_out_kernel(first, second, *outs):
    half = first.shape[1] // len(outs)
    for i, out in enumerate(outs):
        pieces = [part[:, i * half : (i + 1) * half] for part in (first, second)]
        out[...] = jnp.concatenate(pieces, axis=1)


def weights_out(first, second):
    rows, columns = first.shape
    return pl.pallas_call(
        weights_out_kernel,
        out_shape=[jax.ShapeDtypeStruct((rows, columns // 2), F32)] * 4,
        compiler_params=PARAMS,
    )(first, second)


def line_buckets(buckets, span_rows, table_rows):
    place = jnp.arange(2 * LANES, dtype=jnp.int32)
    place = jnp.where(place < LANES, place, place - 2 * LANES)
    distance = jnp.arange(3, dtype=jnp.int32)[:, None] * span_rows - place[None, :]
    known = buckets.shape[0]
    hits = distance[:, :, None] == jnp.arange(known, dtype=jnp.int32)
    bucket = jnp.sum(jnp.where(hits, buckets, 0), axis=-1)
    bucket = jnp.where(distance >= known, table_rows - 1, bucket)
    onehot = bucket[:, :, None] == jnp.arange(table_rows, dtype=jnp.int32)
    return (onehot & (distance >= 0)[:, :, None]).astype(F32), distance >= 0


def bias_lines(table, onehot, valid, pair):
    heads = table.shape[1]
    lines = jnp.einsum("kmb,bh->hkm", onehot, table, precision=PRECISE)
    lines = jnp.where(valid[None], lines, MASKED)
    last = jnp.broadcast_to(table[-1][:, None, None], (heads, 1, lines.shape[2]))
    lines = jnp.concatenate((lines, last), axis=1)
    return lines.reshape(heads // pair, pair * 4, lines.shape[2])


def table_gradient(lines, onehot, heads):
    lines = lines.reshape(heads, 4, lines.shape[2])
    grads = jnp.einsum("hkm,kmb->bh", lines[:, :3], onehot, precision=PRECISE)
    return grads.at[-1].add(jnp.sum(lines[:, 3], axis=-1))


def block_kinds(span_order, first_span, query_spans):
    own = lax.dynamic_slice_in_dim(span_order, first_span, query_spans, 0)
    apart = own[:, None] - span_order[None, :]
    kinds = jnp.where(apart < 0, 0, jnp.where(apart > 2, 4, apart + 1))
    return kinds.reshape(-1).astype(jnp.int32)


def per_device(
    inputs,
    encoder_states,
    cotangent,
    span_order,
    buckets,
    gain_self,
    self_query,
    self_key,
    self_value,
    self_out,
    gain_cross,
    cross_query,
    cross_key,
    cross_value,
    cross_out,
    gain_feed,
    feed_gate,
    feed_up,
    feed_down,
    bias_table,
):
    shards, slots = lax.axis_size("shard"), lax.axis_size("ctx")
    shard_rows, width = self_query.shape
    down_rows = feed_down.shape[0]
    feed = feed_gate.shape[1]
    quads = slots == 4 and shards == 8 and shard_rows % 8 == 0 and down_rows % 8 == 0
    token_rows = inputs.shape[1]
    heads = bias_table.shape[1]
    head_size = width // heads
    pair = LANES // head_size
    table_rows = bias_table.shape[0]
    span_rows = token_rows // 2
    slot = lax.axis_index("ctx")
    enc_rows = encoder_states.shape[1]

    gains = jnp.stack((gain_self, gain_cross, gain_feed), axis=1)
    gains = jnp.pad(gains, ((0, 0), (0, LANES - gains.shape[1])))
    mine = [
        self_query,
        self_key,
        self_value,
        self_out,
        cross_query,
        cross_key,
        cross_value,
        cross_out,
    ]
    sequence = jnp.concatenate((inputs[0], encoder_states[0]), axis=0)
    if quads:
        core = slot % 2
        first, second, *feed_halves = pack_weights(mine, gains, feed_gate, feed_up, feed_down)
        chip, feed_chip = chip_rows(first, second), chip_rows(*feed_halves)
        joint = tied(*z_gather(chip), ctx_gather(sequence, quads), feed_chip)
        *arrived, sequence, feed_chip = joint
        feed_in = z_gather(feed_chip)
        parts = z_ordered(chip, arrived)
        parts = plane_gathered_first(*parts, *plane_first(*parts))
        left_in, right_in, *feed_in = tied(*plane_second(*parts), *feed_in)
        feed_parts = z_ordered(feed_chip, feed_in)
        own, *feed_parts = tied(plane_gathered(*parts, left_in, right_in), *feed_parts)
        other = swap(own, 1)
        feed_in = plane_first(*feed_parts)
        first, second = jnp.where(core == 0, own, other), jnp.where(core == 0, other, own)
    else:
        first = jnp.concatenate((*mine[:4], gains), axis=1)
        first = lax.all_gather(first, BOTH, axis=0, tiled=True)
        second = lax.all_gather(jnp.concatenate(mine[4:], axis=1), BOTH, axis=0, tiled=True)
        core = jnp.int32(0)
        feed_own = lax.all_gather(feed_gate, BOTH, axis=0, tiled=True)
        feed_other = lax.all_gather(feed_up, BOTH, axis=0, tiled=True)
        w_down = lax.all_gather(feed_down, BOTH, axis=0, tiled=True)
        down_own, down_other = w_down[:, : width // 2], w_down[:, width // 2 :]
        sequence = ctx_gather(sequence, quads)
    w_query, w_key_value, w_out = (
        first[:, :width],
        first[:, width : 3 * width],
        first[:, 3 * width : 4 * width],
    )
    w_cross_query, w_cross_key_value, w_cross_out = (
        second[:, :width],
        second[:, width : 3 * width],
        second[:, 3 * width : 4 * width],
    )
    gain_rows = first[:, 4 * width :].T.astype(F32)
    g_self, g_cross, g_feed = gain_rows[0], gain_rows[1], gain_rows[2]

    def by_core(own, other):
        return jnp.where(core == 0, own, other), jnp.where(core == 0, other, own)

    sequence = sequence.reshape(slots, token_rows + enc_rows, width)
    tokens_all = sequence[:, :token_rows].reshape(slots * token_rows, width).astype(F32)
    encoded = sequence[:, token_rows:].reshape(slots * enc_rows, width)

    onehot, valid = line_buckets(buckets, span_rows, table_rows)
    lines = bias_lines(bias_table, onehot, valid, pair)
    kinds = block_kinds(span_order, slot * 2, 2)

    tokens = inputs[0].astype(F32)
    unit_all = tokens_all * inverse_norm(tokens_all)
    normed_all = (unit_all * g_self).astype(BF16)
    inverse_self = inverse_norm(tokens)
    unit_self = tokens * inverse_self
    normed_self = (unit_self * g_self).astype(BF16)
    queries = project(normed_self, w_query).astype(BF16)
    keys_values = project(normed_all, w_key_value).astype(BF16)
    if quads:
        queries, *feed_in = tied(queries, *feed_in)
        feed_parts = plane_gathered_first(*feed_parts, *feed_in)
        queries, *feed_parts = tied(queries, *feed_parts)
        feed_in = plane_second(*feed_parts)
    probs, attended = self_forward(kinds, queries, keys_values, lines, span_rows, head_size)
    after_self = tokens + project(attended, w_out)
    inverse_cross = inverse_norm(after_self)
    unit_cross = after_self * inverse_cross
    normed_cross = (unit_cross * g_cross).astype(BF16)
    cross_q = project(normed_cross, w_cross_query).astype(BF16)
    cross_kv = project(encoded, w_cross_key_value).astype(BF16)
    if quads:
        cross_q, *feed_in = tied(cross_q, *feed_in)
        cross_q, feed_own = tied(cross_q, plane_gathered(*feed_parts, *feed_in))
        feed_other = swap(feed_own, 1)
    cross_probs, cross_att = cross_forward(cross_q, cross_kv, head_size)
    after_cross = after_self + project(cross_att, w_cross_out)
    inverse_feed = inverse_norm(after_cross)
    unit_feed = after_cross * inverse_feed
    normed_feed = (unit_feed * g_feed).astype(BF16)
    if quads:
        down_own, down_other = (
            move_tiles(
                part[:, feed:].reshape(shards * slots, shard_rows, -1), down_rows, width // 2, False
            ).reshape(feed, width // 2)
            for part in (feed_own, feed_other)
        )
        feed_own, feed_other = feed_own[:, :feed], feed_other[:, :feed]
    gate_pre, up_pre = by_core(project(normed_feed, feed_own), project(normed_feed, feed_other))
    gated, gated_pull = jax.vjp(
        lambda first, second: jax.nn.gelu(first, approximate=True) * second, gate_pre, up_pre
    )
    hidden = gated.astype(BF16)
    from_feed = by_core(project(hidden, down_own), project(hidden, down_other))
    outputs = (after_cross + jnp.concatenate(from_feed, axis=1)).astype(BF16)

    grad_out = cotangent[0]
    outer = grad_out.astype(F32)
    half = width // 2
    out_keep, out_send = by_core(grad_out[:, :half], grad_out[:, half:])
    if quads:
        lefts = swap(
            jnp.concatenate(
                (attended, normed_cross, cross_att, normed_feed, hidden, out_send), axis=1
            ),
            1,
        )

    def pair_sum(left, left_in, right, right_in):
        return outer_sum(
            jnp.concatenate((left, left_in), axis=0), jnp.concatenate((right, right_in), axis=0)
        ).astype(BF16)

    grad_hidden = project_back(out_keep, down_own) + project_back(out_send, down_other)
    grad_gate, grad_up = gated_pull(grad_hidden)
    grad_gate, grad_up = grad_gate.astype(BF16), grad_up.astype(BF16)
    keep, sent = by_core(grad_gate, grad_up)
    if quads:
        arrived = swap(sent, 1)
    grad_normed = project_back(keep, feed_own) + project_back(sent, feed_other)
    gain_feed_grad = jnp.sum(grad_normed * unit_feed, axis=0)
    grad_cross_out = outer + norm_back(after_cross, inverse_feed, g_feed, grad_normed)
    grad_low_cross = grad_cross_out.astype(BF16)
    grad_att = project_back(grad_low_cross, w_cross_out).astype(BF16)
    if quads:
        base = 4 * width
        down_part = pair_sum(hidden, lefts[:, base : base + feed], out_keep, lefts[:, base + feed :])
        down_part = move_tiles(
            down_part.reshape(shards * slots, down_rows, width // 2),
            shard_rows,
            down_rows * width // 2 // shard_rows,
            True,
        ).reshape(width, -1)
        cut = (feed + down_part.shape[1]) // 2
        feed_lefts = (normed_feed, lefts[:, 3 * width : 4 * width])
        feed_left = pair_sum(*feed_lefts, keep[:, :cut], arrived[:, :cut])
        feed_right = pair_sum(*feed_lefts, keep[:, cut:], arrived[:, cut:])
        feed_right = jnp.concatenate((feed_right, down_part), axis=1)
        grad_att, *feed_sends = tied(grad_att, *plane_sends(feed_left, feed_right))
        feed_in = plane_first(*feed_sends[:2])
    else:
        own_down = scatter_sum(outer_sum(hidden, grad_out).astype(BF16))
        own_gate = scatter_sum(outer_sum(normed_feed, grad_gate).astype(BF16))
        own_up = scatter_sum(outer_sum(normed_feed, grad_up).astype(BF16))

    groups = width // LANES
    half_groups = groups // 2 if quads else groups

    def scalars_at(kind_scalars, group):
        return jnp.concatenate((kind_scalars, jnp.reshape(group, (1,)).astype(jnp.int32)))

    def in_order(kept, sent, axis):
        if not quads:
            return kept
        first, second = jnp.where(core == 0, kept, sent), jnp.where(core == 0, sent, kept)
        return jnp.concatenate((first, second), axis=axis)

    def attention_sums(kept, arrived, result, lefts_q, lefts_o, keys_from):
        half = width // 2
        left = jnp.concatenate(
            (
                pair_sum(*lefts_q, kept[0], arrived[0][:, :half]),
                pair_sum(*lefts_o, result, arrived[0][:, half:]),
            ),
            axis=1,
        )
        keys_values_sum = add_low(kept[1], arrived[1])
        right = jnp.concatenate((keys_values_sum[0], keys_values_sum[1]), axis=1)
        return left, outer_sum(keys_from, right).astype(BF16)

    none = jnp.zeros((0,), jnp.int32)
    if quads:
        result_keep, result_send = core_halves(grad_low_cross)
        sent = cross_backward(
            scalars_at(none, (1 - core) * half_groups),
            half_groups,
            cross_q,
            grad_att,
            cross_kv,
            cross_probs,
            head_size,
        )
        arrived = (
            swap(jnp.concatenate((sent[0], result_send), axis=1), 1),
            swap(sent[1], 1),
        )
        grad_att, *sent = tied(grad_att, *sent)
    kept = cross_backward(
        scalars_at(none, core * half_groups if quads else jnp.int32(0)),
        half_groups,
        cross_q,
        grad_att,
        cross_kv,
        cross_probs,
        head_size,
    )
    if not quads:
        sent = kept
    grad_cq = in_order(kept[0], sent[0], 1)
    grad_normed = project_back(grad_cq, w_cross_query)
    gain_cross_grad = jnp.sum(grad_normed * unit_cross, axis=0)
    grad_self_out = grad_cross_out + norm_back(after_self, inverse_cross, g_cross, grad_normed)
    grad_low_self = grad_self_out.astype(BF16)
    grad_att = project_back(grad_low_self, w_out).astype(BF16)
    cross_kept, cross_sent = kept[1], sent[1]

    if quads:
        cross_parts = attention_sums(
            kept,
            arrived,
            result_keep,
            (normed_cross, lefts[:, width : 2 * width]),
            (cross_att, lefts[:, 2 * width : 3 * width]),
            encoded,
        )
        grad_att, *cross_sends = tied(grad_att, *plane_sends(*cross_parts))
        cross_in = plane_first(*cross_sends[:2])
        result_keep, result_send = core_halves(grad_low_self)
        sent = self_backward(
            scalars_at(kinds, (1 - core) * half_groups),
            half_groups,
            queries,
            grad_att,
            keys_values,
            probs,
            span_rows,
            head_size,
        )
        arrived = (
            swap(jnp.concatenate((sent[0], result_send), axis=1), 1),
            swap(sent[1], 1),
        )
        joint = tied(grad_att, *feed_in, *sent)
        grad_att, feed_in, sent = joint[0], joint[1:3], joint[3:]
        feed_sends = plane_second_sends(feed_sends[2], feed_in[0], feed_sends[3], feed_in[1])
        grad_att, *feed_sends = tied(grad_att, *feed_sends)
        feed_in = plane_second(*feed_sends[:2])
    kept = self_backward(
        scalars_at(kinds, core * half_groups if quads else jnp.int32(0)),
        half_groups,
        queries,
        grad_att,
        keys_values,
        probs,
        span_rows,
        head_size,
    )
    if not quads:
        sent = kept
    if quads:
        joint = tied(*feed_in, *cross_in, *kept)
        feed_in, cross_in, kept = joint[:2], joint[2:4], joint[4:]
        cross_sends = plane_second_sends(cross_sends[2], cross_in[0], cross_sends[3], cross_in[1])
        joint = tied(*cross_sends, *kept)
        cross_sends, kept = joint[:4], joint[4:]
        cross_in = plane_second(*cross_sends[:2])
        partner = lax.dynamic_slice_in_dim(normed_all, (slot ^ 1) * token_rows, token_rows, 0)
        self_parts = attention_sums(
            kept,
            arrived,
            result_keep,
            (normed_self, partner),
            (attended, lefts[:, :width]),
            normed_all,
        )
        joint = tied(*plane_sends(*self_parts), *cross_in, cross_kept, *kept)
        self_sends, cross_in, (cross_kept, *kept) = joint[:4], joint[4:6], joint[6:]
        first_plane = jnp.concatenate(
            (
                plane_sum(feed_sends[2], feed_in[0], feed_sends[3], feed_in[1]),
                plane_sum(cross_sends[2], cross_in[0], cross_sends[3], cross_in[1]),
            ),
            axis=2,
        )
        first_sends = z_sends(first_plane)
        self_in = plane_first(*self_sends[:2])
        first_in = z_swaps(first_sends)
    grad_q = in_order(kept[0], sent[0], 1)
    part_kv = in_order(kept[1], sent[1], 2)
    part_kv = jnp.concatenate((part_kv[0], part_kv[1]), axis=1)
    part_ckv = in_order(cross_kept, cross_sent, 2)
    part_ckv = jnp.concatenate((part_ckv[0], part_ckv[1]), axis=1)
    grad_lines = in_order(kept[2], sent[2], 0)
    grad_kv_normed = project_back(part_kv, w_key_value)
    grad_q_normed = project_back(grad_q, w_query)
    gain_self_grad = jnp.sum(grad_kv_normed * unit_all, axis=0) + jnp.sum(
        grad_q_normed * unit_self, axis=0
    )
    to_encoder = project_back(part_ckv, w_cross_key_value).astype(BF16)
    to_inputs = grad_kv_normed.astype(BF16)
    if quads:
        joint = tied(*self_in, gain_self_grad, grad_lines)
        self_in, (gain_self_grad, grad_lines) = joint[:2], joint[2:]
        self_sends = plane_second_sends(self_sends[2], self_in[0], self_sends[3], self_in[1])
        self_in = plane_second(*self_sends[:2])
    else:
        cross_query_grad = scatter_sum(outer_sum(normed_cross, grad_cq).astype(BF16))
        cross_out_grad = scatter_sum(outer_sum(cross_att, grad_low_cross).astype(BF16))
        cross_key_grad = scatter_sum(outer_sum(encoded, cross_kept[0]).astype(BF16))
        cross_value_grad = scatter_sum(outer_sum(encoded, cross_kept[1]).astype(BF16))
        query_grad = scatter_sum(outer_sum(normed_self, grad_q).astype(BF16))
        self_out_grad = scatter_sum(outer_sum(attended, grad_low_self).astype(BF16))
        key_grad = scatter_sum(outer_sum(normed_all, kept[1][0]).astype(BF16))
        value_grad = scatter_sum(outer_sum(normed_all, kept[1][1]).astype(BF16))
    table_part = table_gradient(grad_lines, onehot, heads)
    small = jnp.concatenate(
        (gain_self_grad, gain_cross_grad, gain_feed_grad, table_part.reshape(-1))
    )
    tile = 8 * LANES
    extent = small.shape[0]
    small = jnp.pad(small, (0, -extent % tile)).reshape(-1, LANES)
    if quads:
        joint = tied(*self_in, *first_in, small_plane_sum(small), to_encoder, to_inputs)
        self_in, first_in = joint[:2], joint[2 : 1 + len(first_sends)]
        small, to_encoder, to_inputs = joint[1 + len(first_sends) :]
        self_sends = z_sends(
            plane_sum(self_sends[2], self_in[0], self_sends[3], self_in[1])
        )
        self_in = z_swaps(self_sends)
        first, second = between_cores(z_total(first_sends[0], first_in))
        split = first.shape[1] - 2 * width
        own_gate, own_up, own_down = feed_out(
            first[:, :split], second[:, :split], feed, down_rows, width
        )
        cross_query_grad, cross_out_grad, cross_key_grad, cross_value_grad = weights_out(
            first[:, split:], second[:, split:]
        )
        small = small_z_sum(small)
    else:
        small = lax.psum(small, BOTH)
    encoder_grad = ctx_scatter_sum(to_encoder, quads)
    to_inputs = ctx_scatter_sum(to_inputs, quads)
    if quads:
        small, encoder_grad, to_inputs, *self_in = tied(small, encoder_grad, to_inputs, *self_in)
        query_grad, self_out_grad, key_grad, value_grad = weights_out(
            *between_cores(z_total(self_sends[0], self_in))
        )
    grad_normed = grad_q_normed + to_inputs
    input_grad = grad_self_out + norm_back(tokens, inverse_self, g_self, grad_normed)
    small = small.reshape(-1)
    position = lax.axis_index(BOTH) * shard_rows
    own_gains = [
        lax.dynamic_slice_in_dim(small, i * width + position, shard_rows, 0) for i in range(3)
    ]
    table_total = small[3 * width : extent].reshape(table_rows, heads)
    return (
        outputs[None],
        input_grad.astype(BF16)[None],
        encoder_grad.astype(BF16)[None],
        own_gains[0],
        query_grad,
        key_grad,
        value_grad,
        self_out_grad,
        own_gains[1],
        cross_query_grad,
        cross_key_grad,
        cross_value_grad,
        cross_out_grad,
        own_gains[2],
        own_gate,
        own_up,
        own_down,
        table_total,
    )


def solution(mesh):
    in_specs = (
        P("shard", "ctx", None),
        P("shard", "ctx", None),
        P("shard", "ctx", None),
        P(),
        P(),
        P(("shard", "ctx")),
        P(("shard", "ctx"), None),
        P(("shard", "ctx"), None),
        P(("shard", "ctx"), None),
        P(("shard", "ctx"), None),
        P(("shard", "ctx")),
        P(("shard", "ctx"), None),
        P(("shard", "ctx"), None),
        P(("shard", "ctx"), None),
        P(("shard", "ctx"), None),
        P(("shard", "ctx")),
        P(("shard", "ctx"), None),
        P(("shard", "ctx"), None),
        P(("shard", "ctx"), None),
        P(),
    )
    out_specs = (
        P("shard", "ctx", None),
        P("shard", "ctx", None),
        P("shard", "ctx", None),
        P(("shard", "ctx")),
        P(("shard", "ctx"), None),
        P(("shard", "ctx"), None),
        P(("shard", "ctx"), None),
        P(("shard", "ctx"), None),
        P(("shard", "ctx")),
        P(("shard", "ctx"), None),
        P(("shard", "ctx"), None),
        P(("shard", "ctx"), None),
        P(("shard", "ctx"), None),
        P(("shard", "ctx")),
        P(("shard", "ctx"), None),
        P(("shard", "ctx"), None),
        P(("shard", "ctx"), None),
        P(),
    )
    return jax.shard_map(
        per_device, mesh=mesh, in_specs=in_specs, out_specs=out_specs, check_vma=False
    )
```

```python
import functools

import jax
import jax.numpy as jnp
from jax import lax
from jax.experimental import pallas as pl
from jax.experimental.pallas import tpu as pltpu
from jax.sharding import PartitionSpec as P

EPSILON = 1e-06
MASKED = -1e30
PRECISE = lax.Precision.HIGHEST
LANES = 128
BOTH = ("shard", "ctx")
F32 = jnp.float32
BF16 = jnp.bfloat16


def inverse_norm(values):
    return lax.rsqrt(jnp.mean(values * values, axis=-1, keepdims=True) + EPSILON)


def norm_back(values, inverse, gain, grads):
    weighted = gain * grads
    middle = jnp.mean(weighted * values, axis=-1, keepdims=True)
    return inverse * weighted - values * (inverse * inverse * inverse) * middle


def project(left, right):
    return jnp.dot(left, right, preferred_element_type=F32)


def project_back(grads, weight):
    return lax.dot_general(grads, weight, (((1,), (1,)), ((), ())), preferred_element_type=F32)


def outer_sum(left, grads):
    return lax.dot_general(left, grads, (((0,), (0,)), ((), ())), preferred_element_type=F32)


def swap(values, mask):
    count = lax.axis_size("shard") * lax.axis_size("ctx")
    return lax.ppermute(values, BOTH, [(i, i ^ mask) for i in range(count)])


def pick(values, index, axis):
    return lax.dynamic_index_in_dim(values, index, axis, keepdims=False)


def paired(first, second, flag):
    joined = jnp.concatenate((first, second), axis=0)
    return jnp.where(flag == 0, joined, jnp.concatenate((second, first), axis=0))


def ctx_gather(values, quads):
    if not quads:
        return lax.all_gather(values, "ctx", axis=0, tiled=True)
    slot = lax.axis_index("ctx")
    far = swap(values, 2)
    near = paired(values, swap(values, 1), slot % 2)
    far = paired(far, swap(far, 1), slot % 2)
    return paired(near, far, slot // 2)


def ctx_scatter_sum(values, quads):
    if not quads:
        return lax.psum_scatter(values, "ctx", scatter_dimension=0, tiled=True).astype(F32)
    slot = lax.axis_index("ctx")
    core, row = slot % 2, slot // 2
    parts = values.reshape(2, 2, values.shape[0] // 4, values.shape[1])
    summed = pick(parts, core, 1).astype(F32) + swap(pick(parts, 1 - core, 1), 1).astype(F32)
    summed = summed.astype(BF16)
    return pick(summed, row, 0).astype(F32) + swap(pick(summed, 1 - row, 0), 2).astype(F32)


def place():
    shard, ctx = lax.axis_index("shard"), lax.axis_index("ctx")
    return ctx % 2, ctx // 2, shard % 2, shard // 2


def add_low(first, second):
    return (first.astype(F32) + second.astype(F32)).astype(BF16)


def by_chip(values):
    layers = lax.axis_size("shard") // 2
    return values.reshape(layers, 2, 2, values.shape[0] // (layers * 4), values.shape[1])


def plane_sends(left, right):
    _, row, column, _ = place()
    left, right = by_chip(left), by_chip(right)
    sends = pick(left, 1 - column, 1), pick(right, 1 - row, 2)
    return sends + (pick(left, column, 1), pick(right, row, 2))


def plane_first(left_out, right_out):
    return swap(left_out, 4), swap(right_out, 2)


def plane_second_sends(left, left_in, right, right_in):
    _, row, column, _ = place()
    left, right = add_low(left, left_in), add_low(right, right_in)
    sends = pick(left, 1 - row, 1), pick(right, 1 - column, 1)
    return sends + (pick(left, row, 1), pick(right, column, 1))


def plane_second(left_out, right_out):
    return swap(left_out, 2), swap(right_out, 4)


def plane_sum(left, left_in, right, right_in):
    return jnp.concatenate((add_low(left, left_in), add_low(right, right_in)), axis=-1)


def z_sends(plane):
    layer = lax.axis_index("shard") // 2
    return [pick(plane, layer ^ step, 0) for step in range(plane.shape[0])]


def z_swaps(parts):
    return [swap(part, 8 * step) for step, part in enumerate(parts) if step]


def z_total(own, arrived):
    total = own.astype(F32)
    for part in arrived:
        total = total + part.astype(F32)
    return total


def between_cores(total):
    core = lax.axis_index("ctx") % 2
    total = total.reshape(2, total.shape[0] // 2, total.shape[1])
    own = pick(total, core, 0)
    other = swap(pick(total, 1 - core, 0).astype(BF16), 1).astype(F32)
    return jnp.where(core == 0, own, other), jnp.where(core == 0, other, own)


def core_halves(values):
    core = lax.axis_index("ctx") % 2
    half = values.shape[1] // 2
    low, high = values[:, :half], values[:, half:]
    return jnp.where(core == 0, low, high), jnp.where(core == 0, high, low)


def chip_rows(first, second):
    core, _, _, _ = place()
    mine, theirs = jnp.where(core == 0, first, second), jnp.where(core == 0, second, first)
    return paired(mine, swap(theirs, 1), core)


def z_gather(chip):
    return [swap(chip, 8 * step) for step in range(1, lax.axis_size("shard") // 2)]


def z_ordered(chip, arrived):
    layer = lax.axis_index("shard") // 2
    stacked = jnp.stack([chip, *arrived])
    stacked = jnp.stack([pick(stacked, layer ^ step, 0) for step in range(stacked.shape[0])])
    half = chip.shape[1] // 2 // LANES * LANES
    return stacked[..., :half], stacked[..., half:]


def joined(mine, theirs, flag, axis):
    low, high = jnp.where(flag == 0, mine, theirs), jnp.where(flag == 0, theirs, mine)
    return jnp.stack((low, high), axis=axis)


def plane_gathered_first(left, right, left_in, right_in):
    _, row, column, _ = place()
    return joined(left, left_in, column, 1), joined(right, right_in, row, 1)


def plane_gathered(left, right, left_in, right_in):
    _, row, column, _ = place()
    left, right = joined(left, left_in, row, 2), joined(right, right_in, column, 1)
    own = jnp.concatenate((left, right), axis=-1)
    return own.reshape(-1, own.shape[-1])


def tied(value, *others):
    return lax.optimization_barrier((value,) + others)


def scatter_sum(values):
    return lax.psum_scatter(values, BOTH, scatter_dimension=0, tiled=True).astype(F32)


def small_plane_sum(values):
    for mask in (1, 2, 4):
        values = values + swap(values, mask)
    return values


def small_z_sum(values):
    arrived = [swap(values, 8 * step) for step in range(1, lax.axis_size("shard") // 2)]
    layer = lax.axis_index("shard") // 2
    stacked = jnp.stack([values] + arrived)
    return sum(pick(stacked, layer ^ step, 0) for step in range(stacked.shape[0]))


def fold(values, rows, columns):
    lead = values.shape[:-2]
    tall, wide = values.shape[-2] // 8, rows // 8
    step = values.shape[-1] // wide
    cut = values.reshape(lead + (tall, 8, values.shape[-1]))
    bands = []
    for band in range(wide):
        bands.append(
            jnp.concatenate(
                [cut[..., t, :, band * step : (band + 1) * step] for t in range(tall)], axis=-1
            )
        )
    return jnp.concatenate(bands, axis=-2)


def unfold(values, rows, columns):
    tall, wide = rows // 8, values.shape[-2] // 8
    step = columns // wide
    out = []
    for t in range(tall):
        out.append(
            jnp.concatenate(
                [
                    values[..., w * 8 : (w + 1) * 8, t * step : (t + 1) * step]
                    for w in range(wide)
                ],
                axis=-1,
            )
        )
    return jnp.concatenate(out, axis=-2)


def head_mask(shape, head_size, head):
    lane = lax.broadcasted_iota(jnp.int32, shape, 1)
    return lane // head_size == head


def pad_keys(source, target, span_rows):
    spans = source.shape[0] // span_rows
    for b in range(spans):
        target[b * LANES : b * LANES + span_rows, :] = source[
            b * span_rows : (b + 1) * span_rows, :
        ]


def skew(values, right):
    width = values.shape[1]
    row = lax.broadcasted_iota(jnp.int32, values.shape, 0)
    for bit in range((values.shape[0] - 1).bit_length()):
        shift = 1 << bit
        moved = pltpu.roll(values, shift if right else width - shift, 1)
        values = jnp.where((row >> bit) & 1 == 1, moved, values)
    return values


def dot_rows(left, right):
    return lax.dot_general(left, right, (((1,), (1,)), ((), ())), preferred_element_type=F32)


def dot_columns(left, right):
    return lax.dot_general(left, right, (((0,), (0,)), ((), ())), preferred_element_type=F32)


def probabilities(scores):
    top = jnp.max(scores, axis=1, keepdims=True)
    raised = jnp.exp(scores - top)
    return raised * (1.0 / jnp.sum(raised, axis=1, keepdims=True))


def self_forward_kernel(
    kind_ref, q_ref, k_ref, v_ref, line_ref, p_ref, o_ref, kp, vp, tables, s_ref, *, span_rows, head_size
):
    @pl.when(pl.program_id(0) == 0)
    def _():
        kp[...] = jnp.zeros(kp.shape, kp.dtype)
        vp[...] = jnp.zeros(vp.shape, vp.dtype)

    pad_keys(k_ref, kp, span_rows)
    pad_keys(v_ref, vp, span_rows)
    pair = LANES // head_size
    spans = k_ref.shape[0] // span_rows
    query_spans = q_ref.shape[0] // span_rows
    inside = lax.broadcasted_iota(jnp.int32, (span_rows, LANES), 1) < span_rows
    out = jnp.zeros(o_ref.shape, F32)
    for h in range(pair):
        tables[0] = jnp.full((span_rows, LANES), MASKED, F32)
        for k in range(4):
            line = jnp.broadcast_to(
                line_ref[0, h * 4 + k : h * 4 + k + 1, :], (span_rows, 2 * LANES)
            )
            if k < 3:
                line = skew(line, True)
            tables[k + 1] = jnp.where(inside, line[:, :LANES], MASKED)
        q = jnp.where(head_mask(q_ref.shape, head_size, h), q_ref[...], jnp.zeros((), BF16))
        s_ref[...] = dot_rows(q, kp[...]) * (head_size**-0.5)
        for a in range(query_spans):
            for b in range(spans):
                rows, columns = pl.ds(a * span_rows, span_rows), pl.ds(b * LANES, LANES)
                s_ref[rows, columns] = s_ref[rows, columns] + tables[kind_ref[a * spans + b]]
        probs = probabilities(s_ref[...]).astype(BF16)
        p_ref[h] = probs
        v = jnp.where(head_mask(vp.shape, head_size, h), vp[...], jnp.zeros((), BF16))
        out = out + jnp.dot(probs, v, preferred_element_type=F32)
    o_ref[...] = out.astype(BF16)


def cross_forward_kernel(q_ref, k_ref, v_ref, p_ref, o_ref, *, head_size):
    out = jnp.zeros(o_ref.shape, F32)
    for h in range(LANES // head_size):
        q = jnp.where(head_mask(q_ref.shape, head_size, h), q_ref[...], jnp.zeros((), BF16))
        probs = probabilities(dot_rows(q, k_ref[...]) * (head_size**-0.5)).astype(BF16)
        p_ref[h] = probs
        v = jnp.where(head_mask(v_ref.shape, head_size, h), v_ref[...], jnp.zeros((), BF16))
        out = out + jnp.dot(probs, v, preferred_element_type=F32)
    o_ref[...] = out.astype(BF16)


def pair_backward(h, q_ref, do_ref, keys, values, p_ref, head_size):
    grads = jnp.where(head_mask(do_ref.shape, head_size, h), do_ref[...], jnp.zeros((), BF16))
    q = jnp.where(head_mask(q_ref.shape, head_size, h), q_ref[...], jnp.zeros((), BF16))
    probs_low = p_ref[h]
    probs = probs_low.astype(F32)
    grad_probs = dot_rows(grads, values)
    delta = jnp.sum(probs * grad_probs, axis=1, keepdims=True)
    grad_scores = (probs * (grad_probs - delta)).astype(BF16)
    k = jnp.where(head_mask(keys.shape, head_size, h), keys, jnp.zeros((), BF16))
    grad_q = jnp.dot(grad_scores, k, preferred_element_type=F32)
    return grad_scores, grad_q, dot_columns(grad_scores, q), dot_columns(probs_low, grads)


def self_backward_kernel(
    kind_ref,
    q_ref,
    do_ref,
    k_ref,
    v_ref,
    p_ref,
    dq_ref,
    dkv_ref,
    line_ref,
    kp,
    vp,
    tables,
    s_ref,
    *,
    span_rows,
    head_size,
):
    @pl.when(pl.program_id(0) == 0)
    def _():
        kp[...] = jnp.zeros(kp.shape, kp.dtype)
        vp[...] = jnp.zeros(vp.shape, vp.dtype)

    pad_keys(k_ref, kp, span_rows)
    pad_keys(v_ref, vp, span_rows)
    pair = LANES // head_size
    spans = k_ref.shape[0] // span_rows
    query_spans = q_ref.shape[0] // span_rows
    scale = head_size**-0.5
    grad_q = jnp.zeros(dq_ref.shape, F32)
    grad_k = jnp.zeros(kp.shape, F32)
    grad_v = jnp.zeros(vp.shape, F32)
    blank = jnp.zeros((span_rows, LANES), F32)
    for h in range(pair):
        scores, part_q, part_k, part_v = pair_backward(
            h, q_ref, do_ref, kp[...], vp[...], p_ref, head_size
        )
        grad_q, grad_k, grad_v = grad_q + part_q, grad_k + part_k, grad_v + part_v
        s_ref[...] = scores.astype(F32)
        tables[...] = jnp.zeros(tables.shape, F32)
        for a in range(query_spans):
            for b in range(spans):
                kind = kind_ref[a * spans + b]
                rows, columns = pl.ds(a * span_rows, span_rows), pl.ds(b * LANES, LANES)
                tables[kind] = tables[kind] + s_ref[rows, columns]
        for k in range(4):
            block = jnp.concatenate((tables[k + 1], blank), axis=1)
            if k < 3:
                block = skew(block, False)
            line_ref[0, h * 4 + k : h * 4 + k + 1, :] = jnp.sum(block, axis=0, keepdims=True)
    dq_ref[...] = (grad_q * scale).astype(BF16)
    grad_k = (grad_k * scale).astype(BF16)
    grad_v = grad_v.astype(BF16)
    for b in range(spans):
        target, source = pl.ds(b * span_rows, span_rows), slice(b * LANES, b * LANES + span_rows)
        dkv_ref[0, target, :] = grad_k[source]
        dkv_ref[1, target, :] = grad_v[source]


def cross_backward_kernel(
    _, q_ref, do_ref, k_ref, v_ref, p_ref, dq_ref, dkv_ref, *, head_size
):
    scale = head_size**-0.5
    grad_q = jnp.zeros(dq_ref.shape, F32)
    grad_k = jnp.zeros(k_ref.shape, F32)
    grad_v = jnp.zeros(v_ref.shape, F32)
    for h in range(LANES // head_size):
        _, part_q, part_k, part_v = pair_backward(
            h, q_ref, do_ref, k_ref[...], v_ref[...], p_ref, head_size
        )
        grad_q, grad_k, grad_v = grad_q + part_q, grad_k + part_k, grad_v + part_v
    dq_ref[...] = (grad_q * scale).astype(BF16)
    dkv_ref[0] = (grad_k * scale).astype(BF16)
    dkv_ref[1] = grad_v.astype(BF16)


PARAMS = pltpu.CompilerParams(vmem_limit_bytes=48 * 1024 * 1024)


def columns_of(rows, offset=0):
    return pl.BlockSpec((rows, LANES), lambda g, *_: (0, g + offset))


def probs_spec(pair, rows, keys):
    return pl.BlockSpec((pair, rows, keys), lambda g, *_: (g, 0, 0))


def lines_spec():
    return pl.BlockSpec((1, 8, 2 * LANES), lambda g, *_: (g, 0, 0))


def self_forward(kinds, queries, keys_values, lines, span_rows, head_size):
    rows, width = queries.shape
    key_rows = keys_values.shape[0]
    groups, pair = width // LANES, LANES // head_size
    padded = key_rows // span_rows * LANES
    return pl.pallas_call(
        functools.partial(self_forward_kernel, span_rows=span_rows, head_size=head_size),
        grid_spec=pltpu.PrefetchScalarGridSpec(
            num_scalar_prefetch=1,
            grid=(groups,),
            in_specs=[
                columns_of(rows),
                columns_of(key_rows),
                columns_of(key_rows, groups),
                lines_spec(),
            ],
            out_specs=[probs_spec(pair, rows, padded), columns_of(rows)],
            scratch_shapes=[
                pltpu.VMEM((padded, LANES), BF16),
                pltpu.VMEM((padded, LANES), BF16),
                pltpu.VMEM((5, span_rows, LANES), F32),
                pltpu.VMEM((rows, padded), F32),
            ],
        ),
        out_shape=[
            jax.ShapeDtypeStruct((groups * pair, rows, padded), BF16),
            jax.ShapeDtypeStruct((rows, width), BF16),
        ],
        compiler_params=PARAMS,
    )(kinds, queries, keys_values, keys_values, lines)


def backward_specs(rows, key_rows, padded, groups, pair):
    def at(offset=0):
        return lambda g, scalars: (0, g + scalars[scalars.shape[0] - 1] + offset)

    ins = [
        pl.BlockSpec((rows, LANES), at()),
        pl.BlockSpec((rows, LANES), at()),
        pl.BlockSpec((key_rows, LANES), at()),
        pl.BlockSpec((key_rows, LANES), at(groups)),
        pl.BlockSpec(
            (pair, rows, padded), lambda g, scalars: (g + scalars[scalars.shape[0] - 1], 0, 0)
        ),
    ]
    outs = [
        pl.BlockSpec((rows, LANES), lambda g, _: (0, g)),
        pl.BlockSpec((2, key_rows, LANES), lambda g, _: (0, 0, g)),
    ]
    return ins, outs


def self_backward(scalars, count, queries, grads, keys_values, probs, span_rows, head_size):
    rows, width = queries.shape
    key_rows = keys_values.shape[0]
    groups, pair = width // LANES, LANES // head_size
    padded = probs.shape[2]
    in_specs, out_specs = backward_specs(rows, key_rows, padded, groups, pair)
    return pl.pallas_call(
        functools.partial(self_backward_kernel, span_rows=span_rows, head_size=head_size),
        grid_spec=pltpu.PrefetchScalarGridSpec(
            num_scalar_prefetch=1,
            grid=(count,),
            in_specs=in_specs,
            out_specs=out_specs + [lines_spec()],
            scratch_shapes=[
                pltpu.VMEM((padded, LANES), BF16),
                pltpu.VMEM((padded, LANES), BF16),
                pltpu.VMEM((5, span_rows, LANES), F32),
                pltpu.VMEM((rows, padded), F32),
            ],
        ),
        out_shape=[
            jax.ShapeDtypeStruct((rows, count * LANES), BF16),
            jax.ShapeDtypeStruct((2, key_rows, count * LANES), BF16),
            jax.ShapeDtypeStruct((count, 8, 2 * LANES), F32),
        ],
        compiler_params=PARAMS,
    )(scalars, queries, grads, keys_values, keys_values, probs)


def cross_backward(scalars, count, queries, grads, keys_values, probs, head_size):
    rows, width = queries.shape
    key_rows = keys_values.shape[0]
    groups, pair = width // LANES, LANES // head_size
    in_specs, out_specs = backward_specs(rows, key_rows, key_rows, groups, pair)
    return pl.pallas_call(
        functools.partial(cross_backward_kernel, head_size=head_size),
        grid_spec=pltpu.PrefetchScalarGridSpec(
            num_scalar_prefetch=1, grid=(count,), in_specs=in_specs, out_specs=out_specs
        ),
        out_shape=[
            jax.ShapeDtypeStruct((rows, count * LANES), BF16),
            jax.ShapeDtypeStruct((2, key_rows, count * LANES), BF16),
        ],
        compiler_params=PARAMS,
    )(scalars, queries, grads, keys_values, keys_values, probs)


def cross_forward(queries, keys_values, head_size):
    rows, width = queries.shape
    key_rows = keys_values.shape[0]
    groups, pair = width // LANES, LANES // head_size
    return pl.pallas_call(
        functools.partial(cross_forward_kernel, head_size=head_size),
        grid=(groups,),
        in_specs=[columns_of(rows), columns_of(key_rows), columns_of(key_rows, groups)],
        out_specs=[probs_spec(pair, rows, key_rows), columns_of(rows)],
        out_shape=[
            jax.ShapeDtypeStruct((groups * pair, rows, key_rows), BF16),
            jax.ShapeDtypeStruct((rows, width), BF16),
        ],
        compiler_params=PARAMS,
    )(queries, keys_values, keys_values)


def pack_kernel(*refs, pieces):
    parts, gains, outs, sems = refs[:pieces], refs[pieces], refs[pieces + 1 : -1], refs[-1]
    width = parts[0].shape[1]
    half = pieces // 2
    copies = []
    for i, part in enumerate(parts):
        target = outs[i // half].at[:, pl.ds(i % half * width, width)]
        copies.append(pltpu.make_async_copy(part, target, sems.at[i]))
    for copy in copies:
        copy.start()
    for out in outs:
        out[:, half * width :] = gains[...]
    for copy in copies:
        copy.wait()


def pack_feed_kernel(gate, up, down, first, second, sems):
    feed = gate.shape[1]
    copies = []
    for i, (part, out) in enumerate(((gate, first), (up, second))):
        copies.append(pltpu.make_async_copy(part, out.at[:, pl.ds(0, feed)], sems.at[i]))
    for copy in copies:
        copy.start()
    middle = down.shape[1] // 2
    for i, out in enumerate((first, second)):
        piece = down[:, i * middle : (i + 1) * middle].astype(F32)
        out[:, feed:] = fold(piece, out.shape[0], out.shape[1] - feed).astype(out.dtype)
    for copy in copies:
        copy.wait()


def pack_weights(parts, gains):
    rows, width = parts[0].shape
    half = len(parts) // 2 * width + gains.shape[1]
    far, near = pl.BlockSpec(memory_space=pltpu.HBM), pl.BlockSpec(memory_space=pltpu.VMEM)
    return pl.pallas_call(
        functools.partial(pack_kernel, pieces=len(parts)),
        in_specs=[far] * len(parts) + [near],
        out_specs=[near] * 2,
        out_shape=[jax.ShapeDtypeStruct((rows, half), gains.dtype)] * 2,
        scratch_shapes=[pltpu.SemaphoreType.DMA((len(parts),))],
        compiler_params=PARAMS,
    )(*parts, gains)


def pack_feed(gate, up, down):
    rows = gate.shape[0]
    half = gate.shape[1] + down.size // 2 // rows
    far, near = pl.BlockSpec(memory_space=pltpu.HBM), pl.BlockSpec(memory_space=pltpu.VMEM)
    return pl.pallas_call(
        pack_feed_kernel,
        in_specs=[far, far, near],
        out_specs=[near] * 2,
        out_shape=[jax.ShapeDtypeStruct((rows, half), gate.dtype)] * 2,
        scratch_shapes=[pltpu.SemaphoreType.DMA((2,))],
        compiler_params=PARAMS,
    )(gate, up, down)


def move_kernel(in_ref, out_ref, *, folding):
    move = fold if folding else unfold
    for i in range(in_ref.shape[0]):
        moved = move(in_ref[i].astype(F32), out_ref.shape[1], out_ref.shape[2])
        out_ref[i] = moved.astype(out_ref.dtype)


def move_tiles(values, rows, columns, folding):
    blocks = values.shape[0]
    step = 8 if blocks % 8 == 0 else 1
    return pl.pallas_call(
        functools.partial(move_kernel, folding=folding),
        grid=(blocks // step,),
        in_specs=[pl.BlockSpec((step,) + values.shape[1:], lambda g: (g, 0, 0))],
        out_specs=pl.BlockSpec((step, rows, columns), lambda g: (g, 0, 0)),
        out_shape=jax.ShapeDtypeStruct((blocks, rows, columns), values.dtype),
        compiler_params=PARAMS,
    )(values)


def feed_out_kernel(first, second, gate, up, down):
    feed = gate.shape[1]
    gate[...] = first[:, :feed]
    up[...] = second[:, :feed]
    rows, width = down.shape
    parts = [unfold(part[:, feed:], rows, width // 2) for part in (first, second)]
    down[...] = jnp.concatenate(parts, axis=1)


def feed_out(first, second, feed, down_rows, width):
    rows = first.shape[0]
    return pl.pallas_call(
        feed_out_kernel,
        out_shape=[
            jax.ShapeDtypeStruct((rows, feed), F32),
            jax.ShapeDtypeStruct((rows, feed), F32),
            jax.ShapeDtypeStruct((down_rows, width), F32),
        ],
        compiler_params=PARAMS,
    )(first, second)


def weights_out_kernel(first, second, *outs):
    half = first.shape[1] // len(outs)
    for i, out in enumerate(outs):
        pieces = [part[:, i * half : (i + 1) * half] for part in (first, second)]
        out[...] = jnp.concatenate(pieces, axis=1)


def weights_out(first, second):
    rows, columns = first.shape
    return pl.pallas_call(
        weights_out_kernel,
        out_shape=[jax.ShapeDtypeStruct((rows, columns // 2), F32)] * 4,
        compiler_params=PARAMS,
    )(first, second)


def line_buckets(buckets, span_rows, table_rows):
    place = jnp.arange(2 * LANES, dtype=jnp.int32)
    place = jnp.where(place < LANES, place, place - 2 * LANES)
    distance = jnp.arange(3, dtype=jnp.int32)[:, None] * span_rows - place[None, :]
    known = buckets.shape[0]
    hits = distance[:, :, None] == jnp.arange(known, dtype=jnp.int32)
    bucket = jnp.sum(jnp.where(hits, buckets, 0), axis=-1)
    bucket = jnp.where(distance >= known, table_rows - 1, bucket)
    onehot = bucket[:, :, None] == jnp.arange(table_rows, dtype=jnp.int32)
    return (onehot & (distance >= 0)[:, :, None]).astype(F32), distance >= 0


def bias_lines(table, onehot, valid, pair):
    heads = table.shape[1]
    lines = jnp.einsum("kmb,bh->hkm", onehot, table, precision=PRECISE)
    lines = jnp.where(valid[None], lines, MASKED)
    last = jnp.broadcast_to(table[-1][:, None, None], (heads, 1, lines.shape[2]))
    lines = jnp.concatenate((lines, last), axis=1)
    return lines.reshape(heads // pair, pair * 4, lines.shape[2])


def table_gradient(lines, onehot, heads):
    lines = lines.reshape(heads, 4, lines.shape[2])
    grads = jnp.einsum("hkm,kmb->bh", lines[:, :3], onehot, precision=PRECISE)
    return grads.at[-1].add(jnp.sum(lines[:, 3], axis=-1))


def block_kinds(span_order, first_span, query_spans):
    own = lax.dynamic_slice_in_dim(span_order, first_span, query_spans, 0)
    apart = own[:, None] - span_order[None, :]
    kinds = jnp.where(apart < 0, 0, jnp.where(apart > 2, 4, apart + 1))
    return kinds.reshape(-1).astype(jnp.int32)


def per_device(
    inputs,
    encoder_states,
    cotangent,
    span_order,
    buckets,
    gain_self,
    self_query,
    self_key,
    self_value,
    self_out,
    gain_cross,
    cross_query,
    cross_key,
    cross_value,
    cross_out,
    gain_feed,
    feed_gate,
    feed_up,
    feed_down,
    bias_table,
):
    shards, slots = lax.axis_size("shard"), lax.axis_size("ctx")
    shard_rows, width = self_query.shape
    down_rows = feed_down.shape[0]
    feed = feed_gate.shape[1]
    quads = slots == 4 and shards == 8 and shard_rows % 8 == 0 and down_rows % 8 == 0
    token_rows = inputs.shape[1]
    heads = bias_table.shape[1]
    head_size = width // heads
    pair = LANES // head_size
    table_rows = bias_table.shape[0]
    span_rows = token_rows // 2
    slot = lax.axis_index("ctx")
    enc_rows = encoder_states.shape[1]

    gains = jnp.stack((gain_self, gain_cross, gain_feed), axis=1)
    gains = jnp.pad(gains, ((0, 0), (0, LANES - gains.shape[1])))
    mine = [
        self_query,
        self_key,
        self_value,
        self_out,
        cross_query,
        cross_key,
        cross_value,
        cross_out,
    ]
    sequence = jnp.concatenate((inputs[0], encoder_states[0]), axis=0)
    if quads:
        core = slot % 2
        chip = chip_rows(*pack_weights(mine, gains))
        nearest, *arrived = z_gather(chip)
        nearest, *feed_mine, sequence = tied(nearest, feed_gate, feed_up, feed_down, sequence)
        feed_chip = chip_rows(*pack_feed(*feed_mine))
        joint = tied(nearest, *arrived, ctx_gather(sequence, quads), feed_chip)
        *arrived, sequence, feed_chip = joint
        feed_in = z_gather(feed_chip)
        parts = z_ordered(chip, arrived)
        parts = plane_gathered_first(*parts, *plane_first(*parts))
        left_in, right_in, *feed_in = tied(*plane_second(*parts), *feed_in)
        feed_parts = z_ordered(feed_chip, feed_in)
        own, *feed_parts = tied(plane_gathered(*parts, left_in, right_in), *feed_parts)
        other = swap(own, 1)
        feed_in = plane_first(*feed_parts)
        first = jnp.where(core == 0, own, other)
    else:
        first = jnp.concatenate((*mine[:4], gains), axis=1)
        first = lax.all_gather(first, BOTH, axis=0, tiled=True)
        second = lax.all_gather(jnp.concatenate(mine[4:], axis=1), BOTH, axis=0, tiled=True)
        core = jnp.int32(0)
        feed_own = lax.all_gather(feed_gate, BOTH, axis=0, tiled=True)
        feed_other = lax.all_gather(feed_up, BOTH, axis=0, tiled=True)
        w_down = lax.all_gather(feed_down, BOTH, axis=0, tiled=True)
        down_own, down_other = w_down[:, : width // 2], w_down[:, width // 2 :]
        sequence = ctx_gather(sequence, quads)
    w_query, w_key_value, w_out = (
        first[:, :width],
        first[:, width : 3 * width],
        first[:, 3 * width : 4 * width],
    )
    gain_rows = first[:, 4 * width :].T.astype(F32)
    g_self, g_cross, g_feed = gain_rows[0], gain_rows[1], gain_rows[2]

    def by_core(own, other):
        return jnp.where(core == 0, own, other), jnp.where(core == 0, other, own)

    sequence = sequence.reshape(slots, token_rows + enc_rows, width)
    tokens_all = sequence[:, :token_rows].reshape(slots * token_rows, width).astype(F32)
    encoded = sequence[:, token_rows:].reshape(slots * enc_rows, width)

    onehot, valid = line_buckets(buckets, span_rows, table_rows)
    lines = bias_lines(bias_table, onehot, valid, pair)
    kinds = block_kinds(span_order, slot * 2, 2)

    tokens = inputs[0].astype(F32)
    unit_all = tokens_all * inverse_norm(tokens_all)
    normed_all = (unit_all * g_self).astype(BF16)
    inverse_self = inverse_norm(tokens)
    unit_self = tokens * inverse_self
    normed_self = (unit_self * g_self).astype(BF16)
    queries = project(normed_self, w_query).astype(BF16)
    keys_values = project(normed_all, w_key_value).astype(BF16)
    if quads:
        queries, keys_values, *feed_in = tied(queries, keys_values, *feed_in)
        feed_parts = plane_gathered_first(*feed_parts, *feed_in)
        queries, *feed_parts = tied(queries, *feed_parts)
        feed_in = plane_second(*feed_parts)
    probs, attended = self_forward(kinds, queries, keys_values, lines, span_rows, head_size)
    if quads:
        attended, own, other = tied(attended, own, other)
        second = jnp.where(core == 0, other, own)
    w_cross_query, w_cross_key_value, w_cross_out = (
        second[:, :width],
        second[:, width : 3 * width],
        second[:, 3 * width : 4 * width],
    )
    after_self = tokens + project(attended, w_out)
    inverse_cross = inverse_norm(after_self)
    unit_cross = after_self * inverse_cross
    normed_cross = (unit_cross * g_cross).astype(BF16)
    cross_q = project(normed_cross, w_cross_query).astype(BF16)
    cross_kv = project(encoded, w_cross_key_value).astype(BF16)
    if quads:
        cross_q, cross_kv, *feed_in = tied(cross_q, cross_kv, *feed_in)
        cross_q, feed_own = tied(cross_q, plane_gathered(*feed_parts, *feed_in))
        feed_other = swap(feed_own, 1)
    cross_probs, cross_att = cross_forward(cross_q, cross_kv, head_size)
    after_cross = after_self + project(cross_att, w_cross_out)
    inverse_feed = inverse_norm(after_cross)
    unit_feed = after_cross * inverse_feed
    normed_feed = (unit_feed * g_feed).astype(BF16)
    if quads:
        down_own, down_other = (
            move_tiles(
                part[:, feed:].reshape(shards * slots, shard_rows, -1), down_rows, width // 2, False
            ).reshape(feed, width // 2)
            for part in (feed_own, feed_other)
        )
        feed_own, feed_other = feed_own[:, :feed], feed_other[:, :feed]
    gate_pre, up_pre = by_core(project(normed_feed, feed_own), project(normed_feed, feed_other))
    gated, gated_pull = jax.vjp(
        lambda first, second: jax.nn.gelu(first, approximate=True) * second, gate_pre, up_pre
    )
    hidden = gated.astype(BF16)
    from_feed = by_core(project(hidden, down_own), project(hidden, down_other))
    outputs = (after_cross + jnp.concatenate(from_feed, axis=1)).astype(BF16)

    grad_out = cotangent[0]
    outer = grad_out.astype(F32)
    half = width // 2
    out_keep, out_send = by_core(grad_out[:, :half], grad_out[:, half:])
    if quads:
        lefts = swap(
            jnp.concatenate(
                (attended, normed_cross, cross_att, normed_feed, hidden, out_send), axis=1
            ),
            1,
        )

    def pair_sum(left, left_in, right, right_in):
        return outer_sum(
            jnp.concatenate((left, left_in), axis=0), jnp.concatenate((right, right_in), axis=0)
        ).astype(BF16)

    grad_hidden = project_back(out_keep, down_own) + project_back(out_send, down_other)
    grad_gate, grad_up = gated_pull(grad_hidden)
    grad_gate, grad_up = grad_gate.astype(BF16), grad_up.astype(BF16)
    keep, sent = by_core(grad_gate, grad_up)
    if quads:
        arrived = swap(sent, 1)
    grad_normed = project_back(keep, feed_own) + project_back(sent, feed_other)
    gain_feed_grad = jnp.sum(grad_normed * unit_feed, axis=0)
    grad_cross_out = outer + norm_back(after_cross, inverse_feed, g_feed, grad_normed)
    grad_low_cross = grad_cross_out.astype(BF16)
    grad_att = project_back(grad_low_cross, w_cross_out).astype(BF16)
    if quads:
        base = 4 * width
        down_part = pair_sum(hidden, lefts[:, base : base + feed], out_keep, lefts[:, base + feed :])
        down_part = move_tiles(
            down_part.reshape(shards * slots, down_rows, width // 2),
            shard_rows,
            down_rows * width // 2 // shard_rows,
            True,
        ).reshape(width, -1)
        cut = (feed + down_part.shape[1]) // 2
        feed_lefts = (normed_feed, lefts[:, 3 * width : 4 * width])
        feed_left = pair_sum(*feed_lefts, keep[:, :cut], arrived[:, :cut])
        feed_right = pair_sum(*feed_lefts, keep[:, cut:], arrived[:, cut:])
        feed_right = jnp.concatenate((feed_right, down_part), axis=1)
        grad_att, *feed_sends = tied(grad_att, *plane_sends(feed_left, feed_right))
        feed_in = plane_first(*feed_sends[:2])
    else:
        own_down = scatter_sum(outer_sum(hidden, grad_out).astype(BF16))
        own_gate = scatter_sum(outer_sum(normed_feed, grad_gate).astype(BF16))
        own_up = scatter_sum(outer_sum(normed_feed, grad_up).astype(BF16))

    groups = width // LANES
    half_groups = groups // 2 if quads else groups

    def scalars_at(kind_scalars, group):
        return jnp.concatenate((kind_scalars, jnp.reshape(group, (1,)).astype(jnp.int32)))

    def in_order(kept, sent, axis):
        if not quads:
            return kept
        first, second = jnp.where(core == 0, kept, sent), jnp.where(core == 0, sent, kept)
        return jnp.concatenate((first, second), axis=axis)

    def attention_sums(kept, arrived, result, lefts_q, lefts_o, keys_from):
        half = width // 2
        left = jnp.concatenate(
            (
                pair_sum(*lefts_q, kept[0], arrived[0][:, :half]),
                pair_sum(*lefts_o, result, arrived[0][:, half:]),
            ),
            axis=1,
        )
        keys_values_sum = add_low(kept[1], arrived[1])
        right = jnp.concatenate((keys_values_sum[0], keys_values_sum[1]), axis=1)
        return left, outer_sum(keys_from, right).astype(BF16)

    none = jnp.zeros((0,), jnp.int32)
    if quads:
        result_keep, result_send = core_halves(grad_low_cross)
        sent = cross_backward(
            scalars_at(none, (1 - core) * half_groups),
            half_groups,
            cross_q,
            grad_att,
            cross_kv,
            cross_probs,
            head_size,
        )
        arrived = (
            swap(jnp.concatenate((sent[0], result_send), axis=1), 1),
            swap(sent[1], 1),
        )
        grad_att, *sent = tied(grad_att, *sent)
    kept = cross_backward(
        scalars_at(none, core * half_groups if quads else jnp.int32(0)),
        half_groups,
        cross_q,
        grad_att,
        cross_kv,
        cross_probs,
        head_size,
    )
    if not quads:
        sent = kept
    grad_cq = in_order(kept[0], sent[0], 1)
    grad_normed = project_back(grad_cq, w_cross_query)
    gain_cross_grad = jnp.sum(grad_normed * unit_cross, axis=0)
    grad_self_out = grad_cross_out + norm_back(after_self, inverse_cross, g_cross, grad_normed)
    grad_low_self = grad_self_out.astype(BF16)
    grad_att = project_back(grad_low_self, w_out).astype(BF16)
    cross_kept, cross_sent = kept[1], sent[1]

    if quads:
        cross_parts = attention_sums(
            kept,
            arrived,
            result_keep,
            (normed_cross, lefts[:, width : 2 * width]),
            (cross_att, lefts[:, 2 * width : 3 * width]),
            encoded,
        )
        grad_att, *cross_sends = tied(grad_att, *plane_sends(*cross_parts))
        cross_in = plane_first(*cross_sends[:2])
        result_keep, result_send = core_halves(grad_low_self)
        sent = self_backward(
            scalars_at(kinds, (1 - core) * half_groups),
            half_groups,
            queries,
            grad_att,
            keys_values,
            probs,
            span_rows,
            head_size,
        )
        arrived = (
            swap(jnp.concatenate((sent[0], result_send), axis=1), 1),
            swap(sent[1], 1),
        )
        joint = tied(grad_att, *feed_in, *sent)
        grad_att, feed_in, sent = joint[0], joint[1:3], joint[3:]
        feed_sends = plane_second_sends(feed_sends[2], feed_in[0], feed_sends[3], feed_in[1])
        grad_att, *feed_sends = tied(grad_att, *feed_sends)
        feed_in = plane_second(*feed_sends[:2])
    kept = self_backward(
        scalars_at(kinds, core * half_groups if quads else jnp.int32(0)),
        half_groups,
        queries,
        grad_att,
        keys_values,
        probs,
        span_rows,
        head_size,
    )
    if not quads:
        sent = kept
    if quads:
        joint = tied(*feed_in, *cross_in, *kept)
        feed_in, cross_in, kept = joint[:2], joint[2:4], joint[4:]
        cross_sends = plane_second_sends(cross_sends[2], cross_in[0], cross_sends[3], cross_in[1])
        joint = tied(*cross_sends, *kept)
        cross_sends, kept = joint[:4], joint[4:]
        cross_in = plane_second(*cross_sends[:2])
        partner = lax.dynamic_slice_in_dim(normed_all, (slot ^ 1) * token_rows, token_rows, 0)
        self_parts = attention_sums(
            kept,
            arrived,
            result_keep,
            (normed_self, partner),
            (attended, lefts[:, :width]),
            normed_all,
        )
        joint = tied(*plane_sends(*self_parts), *cross_in, cross_kept, *kept)
        self_sends, cross_in, (cross_kept, *kept) = joint[:4], joint[4:6], joint[6:]
        first_plane = jnp.concatenate(
            (
                plane_sum(feed_sends[2], feed_in[0], feed_sends[3], feed_in[1]),
                plane_sum(cross_sends[2], cross_in[0], cross_sends[3], cross_in[1]),
            ),
            axis=2,
        )
        first_sends = z_sends(first_plane)
        self_in = plane_first(*self_sends[:2])
        first_in = z_swaps(first_sends)
    grad_q = in_order(kept[0], sent[0], 1)
    part_kv = in_order(kept[1], sent[1], 2)
    part_kv = jnp.concatenate((part_kv[0], part_kv[1]), axis=1)
    part_ckv = in_order(cross_kept, cross_sent, 2)
    part_ckv = jnp.concatenate((part_ckv[0], part_ckv[1]), axis=1)
    grad_lines = in_order(kept[2], sent[2], 0)
    grad_kv_normed = project_back(part_kv, w_key_value)
    grad_q_normed = project_back(grad_q, w_query)
    gain_self_grad = jnp.sum(grad_kv_normed * unit_all, axis=0) + jnp.sum(
        grad_q_normed * unit_self, axis=0
    )
    to_encoder = project_back(part_ckv, w_cross_key_value).astype(BF16)
    to_inputs = grad_kv_normed.astype(BF16)
    if quads:
        joint = tied(*self_in, gain_self_grad, grad_lines)
        self_in, (gain_self_grad, grad_lines) = joint[:2], joint[2:]
        self_sends = plane_second_sends(self_sends[2], self_in[0], self_sends[3], self_in[1])
        self_in = plane_second(*self_sends[:2])
    else:
        cross_query_grad = scatter_sum(outer_sum(normed_cross, grad_cq).astype(BF16))
        cross_out_grad = scatter_sum(outer_sum(cross_att, grad_low_cross).astype(BF16))
        cross_key_grad = scatter_sum(outer_sum(encoded, cross_kept[0]).astype(BF16))
        cross_value_grad = scatter_sum(outer_sum(encoded, cross_kept[1]).astype(BF16))
        query_grad = scatter_sum(outer_sum(normed_self, grad_q).astype(BF16))
        self_out_grad = scatter_sum(outer_sum(attended, grad_low_self).astype(BF16))
        key_grad = scatter_sum(outer_sum(normed_all, kept[1][0]).astype(BF16))
        value_grad = scatter_sum(outer_sum(normed_all, kept[1][1]).astype(BF16))
    table_part = table_gradient(grad_lines, onehot, heads)
    small = jnp.concatenate(
        (gain_self_grad, gain_cross_grad, gain_feed_grad, table_part.reshape(-1))
    )
    tile = 8 * LANES
    extent = small.shape[0]
    small = jnp.pad(small, (0, -extent % tile)).reshape(-1, LANES)
    if quads:
        joint = tied(*self_in, *first_in, small_plane_sum(small), to_encoder, to_inputs)
        self_in, first_in = joint[:2], joint[2 : 1 + len(first_sends)]
        small, to_encoder, to_inputs = joint[1 + len(first_sends) :]
        self_sends = z_sends(
            plane_sum(self_sends[2], self_in[0], self_sends[3], self_in[1])
        )
        self_in = z_swaps(self_sends)
        first, second = between_cores(z_total(first_sends[0], first_in))
        split = first.shape[1] - 2 * width
        own_gate, own_up, own_down = feed_out(
            first[:, :split], second[:, :split], feed, down_rows, width
        )
        cross_query_grad, cross_out_grad, cross_key_grad, cross_value_grad = weights_out(
            first[:, split:], second[:, split:]
        )
        small = small_z_sum(small)
    else:
        small = lax.psum(small, BOTH)
    encoder_grad = ctx_scatter_sum(to_encoder, quads)
    to_inputs = ctx_scatter_sum(to_inputs, quads)
    if quads:
        small, encoder_grad, to_inputs, *self_in = tied(small, encoder_grad, to_inputs, *self_in)
        query_grad, self_out_grad, key_grad, value_grad = weights_out(
            *between_cores(z_total(self_sends[0], self_in))
        )
    grad_normed = grad_q_normed + to_inputs
    input_grad = grad_self_out + norm_back(tokens, inverse_self, g_self, grad_normed)
    small = small.reshape(-1)
    position = lax.axis_index(BOTH) * shard_rows
    own_gains = [
        lax.dynamic_slice_in_dim(small, i * width + position, shard_rows, 0) for i in range(3)
    ]
    table_total = small[3 * width : extent].reshape(table_rows, heads)
    return (
        outputs[None],
        input_grad.astype(BF16)[None],
        encoder_grad.astype(BF16)[None],
        own_gains[0],
        query_grad,
        key_grad,
        value_grad,
        self_out_grad,
        own_gains[1],
        cross_query_grad,
        cross_key_grad,
        cross_value_grad,
        cross_out_grad,
        own_gains[2],
        own_gate,
        own_up,
        own_down,
        table_total,
    )


def solution(mesh):
    in_specs = (
        P("shard", "ctx", None),
        P("shard", "ctx", None),
        P("shard", "ctx", None),
        P(),
        P(),
        P(("shard", "ctx")),
        P(("shard", "ctx"), None),
        P(("shard", "ctx"), None),
        P(("shard", "ctx"), None),
        P(("shard", "ctx"), None),
        P(("shard", "ctx")),
        P(("shard", "ctx"), None),
        P(("shard", "ctx"), None),
        P(("shard", "ctx"), None),
        P(("shard", "ctx"), None),
        P(("shard", "ctx")),
        P(("shard", "ctx"), None),
        P(("shard", "ctx"), None),
        P(("shard", "ctx"), None),
        P(),
    )
    out_specs = (
        P("shard", "ctx", None),
        P("shard", "ctx", None),
        P("shard", "ctx", None),
        P(("shard", "ctx")),
        P(("shard", "ctx"), None),
        P(("shard", "ctx"), None),
        P(("shard", "ctx"), None),
        P(("shard", "ctx"), None),
        P(("shard", "ctx")),
        P(("shard", "ctx"), None),
        P(("shard", "ctx"), None),
        P(("shard", "ctx"), None),
        P(("shard", "ctx"), None),
        P(("shard", "ctx")),
        P(("shard", "ctx"), None),
        P(("shard", "ctx"), None),
        P(("shard", "ctx"), None),
        P(),
    )
    return jax.shard_map(
        per_device, mesh=mesh, in_specs=in_specs, out_specs=out_specs, check_vma=False
    )
```
